256 devices in a mesh: dp: 4 (over z_lo), ctx: 64 (over y, z_hi, x, core).
Axes of the slice: x: 4, y: 4, z: 8 (z_hi: 2, z_lo: 4; z = z_hi * 4 + z_lo), core: 2. Of those that a mesh axis runs over, the one named last changes fastest.
Arguments:
- queries: bfloat16 [4, 8192, 1536], P('dp', 'ctx'), may hold values from -16 to 16
- values: bfloat16 [4, 8192, 1536], P('dp', 'ctx'), may hold values from -6 to 6
- out_grad: bfloat16 [4, 8192, 1536], P('dp', 'ctx'), may hold values from -6 to 6
- out_weight: bfloat16 [1536, 1536], replicated, may hold values from -0.15625 to 0.15625
- filter_spec: bfloat16 [2, 8192, 1536], P(None, 'ctx'), may hold values from -6 to 6
Outputs:
- grad_queries: bfloat16 [4, 8192, 1536], P('dp', 'ctx')
- grad_values: bfloat16 [4, 8192, 1536], P('dp', 'ctx')
- grad_filter: float32 [2, 8192, 1536], P(None, 'ctx')
- grad_weight: float32 [1536, 1536], P('ctx')
The draws below stay inside these ranges and needn't reach their ends.
All inputs are finite; a program needn't handle non-finite values.
Results may differ from the reference program's by a relative error of at most 0.014.
Values may be sent and summed in bfloat16 or wider, within the bound.
A program may use at most 128 MiB of HBM per device.

```python
import math
import jax
import jax.numpy as jnp

D = 1536
TOK_DEV = 128
SEQ = 8192
COPIES = 4
N_CTX = 64


def raised(values, own_key, source, target, shards_of, factor):
    def block_of(axis_at):
        return (jnp.arange(values.shape[axis_at]) // (values.shape[axis_at] // shards_of)).reshape((-1,) + (1,) * (values.ndim - 1 - axis_at))

    near = jax.random.permutation(own_key, shards_of)[block_of(target)]
    other_side = (block_of(target) + shards_of // 2) % shards_of
    return jnp.where((block_of(source) == near) | (block_of(source) == other_side), factor * values, values)


def levels(stream_key, extent, shards, smallest, largest):
    factor_of = 1.0
    for axis_at, parts in shards:
        heights = jax.random.uniform(jax.random.fold_in(jax.random.fold_in(stream_key, 6), axis_at), (parts,), jnp.float32, smallest / len(shards), largest / len(shards))
        factor_of = factor_of * jnp.repeat(jnp.exp(heights), extent[axis_at] // parts).reshape((-1,) + (1,) * (len(extent) - 1 - axis_at))
    return factor_of


def noise(key, extent, deviation, limit, split=(), held_as=jnp.bfloat16):
    gain = levels(key, extent, split, -0.22, 0.18) if split else 1.0
    result = jax.random.normal(key, extent, jnp.float32) * deviation * gain
    return jnp.minimum(jnp.maximum(result, -limit), limit).astype(held_as)


def bell_draw_with(stream_key, dims, spread, limit, cuts, heavy, held_as=jnp.bfloat16):
    entries = spread * jax.random.normal(stream_key, dims, jnp.float32)
    if cuts:
        entries = entries * levels(stream_key, dims, cuts, -0.22, 0.18)
    return jnp.clip(raised(entries, jax.random.fold_in(stream_key, 3), *heavy), -limit, limit).astype(held_as)


def setup_inputs(seed: int = 0) -> dict:
    streams_of = jax.random.split(jax.random.key(seed), 6)
    return {
        "queries": bell_draw_with(streams_of[0], (COPIES, SEQ, D), 1.0, 16.0, ((0, 4), (1, 64)), (1, 2, 64, 4.0)),
        "values": noise(streams_of[1], (COPIES, SEQ, D), 1.0, 6.0, ((0, 4), (1, 64))),
        "out_grad": noise(streams_of[2], (COPIES, SEQ, D), 1.0, 6.0, ((0, 4), (1, 64))),
        "out_weight": noise(streams_of[3], (D, D), D ** -0.5, 0.15625),
        "filter_spec": noise(streams_of[4], (2, SEQ, D), 1.0, 6.0, ((1, 64),)),
    }


def to_natural(stacked):
    spectrum = stacked[0] + 1j * stacked[1]
    return spectrum.reshape(N_CTX, TOK_DEV, D).transpose(1, 0, 2).reshape(SEQ, D)

def to_stacked(spectrum):
    ordered = spectrum.reshape(TOK_DEV, N_CTX, D).transpose(1, 0, 2).reshape(SEQ, D)
    return jnp.stack([jnp.real(ordered), jnp.imag(ordered)])

def reference(queries, values, out_grad, out_weight, filter_spec):
    filter_full = to_natural(filter_spec.astype(jnp.float32))
    grad_filter = jnp.zeros((2, SEQ, D), jnp.float32)
    weight_sum = jnp.zeros((D, D), jnp.float32)
    query_grads = []
    value_grads = []
    for copy_index in range(COPIES):
        value_spec = jnp.fft.fft(values[copy_index].astype(jnp.float32), axis=0)
        mixed_rows = jnp.real(jnp.fft.ifft(filter_full * value_spec, axis=0))
        query_float = queries[copy_index].astype(jnp.float32)
        gated_rows = (query_float * mixed_rows).astype(jnp.bfloat16)
        grad_gated = jnp.dot(out_grad[copy_index], out_weight.T, preferred_element_type=jnp.float32)
        query_grads.append((grad_gated * mixed_rows).astype(jnp.bfloat16))
        grad_mixed = grad_gated * query_float
        grad_spec = jnp.fft.fft(grad_mixed, axis=0)
        grad_filter = grad_filter + to_stacked(grad_spec * jnp.conj(value_spec)) / SEQ
        value_grads.append(jnp.real(jnp.fft.ifft(grad_spec * jnp.conj(filter_full), axis=0)).astype(jnp.bfloat16))
        weight_sum = weight_sum + jnp.dot(gated_rows.T, out_grad[copy_index], preferred_element_type=jnp.float32)
    grad_weight = weight_sum * (1.0 / math.sqrt(COPIES * SEQ))
    return (jnp.stack(query_grads), jnp.stack(value_grads), grad_filter, grad_weight)
```

```python
import functools
import math

import jax
import jax.numpy as jnp
import numpy as np
from jax import lax
from jax.experimental import pallas as pl
from jax.experimental.pallas import tpu as pltpu
from jax.sharding import PartitionSpec as P

F32 = jnp.float32
BF16 = jnp.bfloat16
TOK = 128
D = 1536
SEQ = 8192
SLOTS = 33
ROWS = SLOTS * 16
MESH = pl.DeviceIdType.MESH


def slot_of(k):
    if k == 32:
        return 16
    if k % 4 == 0:
        return k // 4
    if k % 4 == 2:
        return 8 + k // 4
    return 17 + k // 4


HELD = [k for k in range(64) if k % 4 == 1 or (k % 2 == 0 and k <= 32)]


def tables():
    r = np.arange(TOK)
    angle = 2.0 * math.pi * ((r[:, None] * r[None, :]) % TOK) / TOK
    c, s = np.cos(angle), np.sin(angle)
    forward = np.block([[c, -s], [s, c]])
    inverse = np.block([[c, s], [-s, c]])

    def halves(m):
        hi = m.astype(np.float32).astype(jnp.bfloat16)
        lo = (m - hi.astype(np.float64)).astype(np.float32).astype(jnp.bfloat16)
        return np.stack([hi, lo])

    twist = np.zeros((2, 40, TOK), np.float32)
    for k in HELD:
        a = 2.0 * math.pi * k * r / SEQ
        twist[0, slot_of(k)] = np.cos(a)
        twist[1, slot_of(k)] = np.sin(a)
    return halves(forward), halves(inverse), twist


def p_add(a, b):
    if a is None:
        return b
    return a if b is None else a + b


def p_sub(a, b):
    if b is None:
        return a
    return -b if a is None else a - b


def c_add(a, b):
    return (p_add(a[0], b[0]), p_add(a[1], b[1]))


def c_sub(a, b):
    return (p_sub(a[0], b[0]), p_sub(a[1], b[1]))


def by_i(a):
    return (p_sub(None, a[1]), a[0])


def p_mul(a, f):
    return None if a is None or f == 0.0 else a * f


def turn(z, k, n):
    k = k % n
    if k == 0:
        return z
    if 4 * k == n:
        return by_i(z)
    if 2 * k == n:
        return c_sub((None, None), z)
    if 4 * k == 3 * n:
        return (z[1], p_sub(None, z[0]))
    c, s = math.cos(2 * math.pi * k / n), math.sin(2 * math.pi * k / n)
    return (
        p_sub(p_mul(z[0], c), p_mul(z[1], s)),
        p_add(p_mul(z[0], s), p_mul(z[1], c)),
    )


def four(z, sign):
    t0, t1 = c_add(z[0], z[2]), c_sub(z[0], z[2])
    t2, t3 = c_add(z[1], z[3]), by_i(c_sub(z[1], z[3]))
    if sign < 0:
        return [c_add(t0, t2), c_sub(t1, t3), c_sub(t0, t2), c_add(t1, t3)]
    return [c_add(t0, t2), c_add(t1, t3), c_sub(t0, t2), c_sub(t1, t3)]


def blocks_forward(get, put):
    t = {}
    for h in range(2):
        for c in range(2):
            for x in range(4):
                v = [get(h, c, y, x) for y in range(4)]
                s02, d02 = v[0] + v[2], v[0] - v[2]
                s13, d13 = v[1] + v[3], v[1] - v[3]
                a = 8 * h + 2 * x + c
                t[0, h, c, x] = (s02 + s13, None)
                t[1, h, c, x] = turn((d02, -d13), -a, 64)
                t[2, h, c, x] = turn((s02 - s13, None), -2 * a, 64)
    for ky in range(3):
        for kh in range(2):
            halves = []
            for c in range(2):
                z = []
                for x in range(4):
                    if kh == 0:
                        z.append(c_add(t[ky, 0, c, x], t[ky, 1, c, x]))
                    else:
                        z.append(turn(c_sub(t[ky, 0, c, x], t[ky, 1, c, x]), -(2 * x + c), 16))
                z = four(z, -1)
                if c == 1:
                    z = [turn(z[kx], -kx, 8) for kx in range(4)]
                halves.append(z)
            for kx in range(4):
                k = ky + 4 * kh + 8 * kx
                put(slot_of(k), c_add(halves[0][kx], halves[1][kx]))
                if ky == 1 or k == 0:
                    put(slot_of(k + 32), c_sub(halves[0][kx], halves[1][kx]))


def blocks_inverse(get, put):
    u = {}
    for ky in range(3):
        for kh in range(2):
            lanes = [[], []]
            for kx in range(4):
                k = ky + 4 * kh + 8 * kx
                z = get(slot_of(k))
                if ky == 1 or k == 0:
                    w = get(slot_of(k + 32))
                    first, second = c_add(z, w), c_sub(z, w)
                else:
                    first, second = z, z
                lanes[0].append(first)
                lanes[1].append(turn(second, kx, 8))
            for c in range(2):
                z = four(lanes[c], 1)
                for x in range(4):
                    u[ky, kh, c, x] = turn(z[x], (2 * x + c) * kh, 16)
    for c in range(2):
        for x in range(4):
            for h in range(2):
                a = 8 * h + 2 * x + c
                join = c_add if h == 0 else c_sub
                u0 = join(u[0, 0, c, x], u[0, 1, c, x])[0]
                u1 = turn(join(u[1, 0, c, x], u[1, 1, c, x]), a, 64)
                u2 = turn(join(u[2, 0, c, x], u[2, 1, c, x]), 2 * a, 64)[0]
                even, odd = u0 + u2, u0 - u2
                put(h, c, 0, x, even + u1[0])
                put(h, c, 1, x, odd - u1[1])
                put(h, c, 2, x, even - u1[0])
                put(h, c, 3, x, odd + u1[1])


def split(v):
    hi = v.astype(BF16)
    return hi, (v - hi.astype(F32)).astype(BF16)


def dot(a, b):
    return jnp.dot(a, b, preferred_element_type=F32)


def dot_t(a, b):
    return lax.dot_general(a, b, (((1,), (1,)), ((), ())), preferred_element_type=F32)


def dot3(hi, lo, m):
    return dot(hi, m[0]) + dot(lo, m[0]) + dot(hi, m[1])


def kernel(
    values, queries, out_grad, weight, filt, m_fwd, m_inv, twist,
    o_query, o_value, o_filter, o_weight,
    w_in, og_x, g_gated, qt, val_t, gm_t, fil_t,
    r1v, r1g, f1, xv, xg, hx, hrev, hs, lhi, llo, spec_v, spec_g, back,
    ymix, ygv, r2m, r2v, mix_t, gv_t, gp, gpx, gs, gr, gfi,
    gat, gat_x, wa, ra0, ra1, sb0, sb1, rb0, rb1, sc, rc, sd, rd,
    s_w, s_ogs, s_ogr, s_gts, s_gtr, s_gps, s_gpr,
    s1vs, s1vr, s1gs, s1gr, s1fs, s1fr,
    s2vs, s2vr, s2gs, s2gr, s2fs, s2fr, s3fs, s3fr,
    sams, samr, savs, savr, sbms, sbmr, sbvs, sbvr,
    sags, sagr, sbgs, sbgr,
    sras, srar, srbs, srbr, srcs, srcr, srds, srdr,
):
    n = lax.axis_index("dp")
    ctx = lax.axis_index("ctx")
    y, h = lax.div(ctx, 16), lax.rem(lax.div(ctx, 8), 2)
    x, c = lax.rem(lax.div(ctx, 2), 4), lax.rem(ctx, 2)
    p, z = y * 4 + x, h * 4 + n
    hc = h * 2 + c
    active = n != 2
    unit = z - (z >= 3).astype(jnp.int32) - (z >= 7).astype(jnp.int32)

    def at(pp, zz, cc):
        return (
            lax.rem(zz, 4),
            lax.div(pp, 4) * 16 + lax.div(zz, 4) * 8 + lax.rem(pp, 4) * 2 + cc,
        )

    def remote(src, dst, ss, rs, dev):
        return pltpu.make_async_remote_copy(
            src_ref=src, dst_ref=dst, send_sem=ss, recv_sem=rs,
            device_id=dev, device_id_type=MESH,
        )

    def local(src, dst, sem):
        pltpu.make_async_copy(src, dst, sem).start()

    def landed(dst, sem):
        pltpu.make_async_copy(dst, dst, sem).wait()

    def left(src, sem):
        pltpu.make_async_copy(src, src, sem).wait()

    def rounds(lo, hi, body):
        lax.fori_loop(lo, hi, lambda i, carry: (body(i), carry)[1], 0)

    def over_p(send):
        rounds(1, 16, lambda i: send(lax.rem(p + i, 16)))

    weight_copy = pltpu.make_async_copy(weight, w_in, s_w)
    weight_copy.start()

    barrier = pltpu.get_barrier_semaphore()

    def greet_p(q):
        pl.semaphore_signal(barrier, inc=1, device_id=at(q, z, c), device_id_type=MESH)

    over_p(greet_p)

    def greet_z(i):
        zz = lax.rem(z + lax.div(i, 2), 8)
        cc = lax.rem(c + lax.rem(i, 2), 2)
        pl.semaphore_signal(barrier, inc=1, device_id=at(p, zz, cc), device_id_type=MESH)

    rounds(1, 16, greet_z)

    def turn_in(src, dst):
        for j in range(D // 128):
            dst[j * 128 : (j + 1) * 128, :] = src[:, j * 128 : (j + 1) * 128].T

    turn_in(values, val_t)
    pl.semaphore_wait(barrier, 30)

    def hop1(src, dst, ss, rs):
        local(src.at[pl.ds(p * 96, 96)], dst.at[p], rs.at[p])
        over_p(
            lambda q: remote(
                src.at[pl.ds(q * 96, 96)], dst.at[p], ss.at[q], rs.at[p], at(q, z, c)
            ).start()
        )

    def hop1_done(src, ss):
        over_p(lambda q: left(src.at[pl.ds(q * 96, 96)], ss.at[q]))

    hop1(val_t, r1v, s1vs, s1vr)

    other = at(p, z, 1 - c)
    lanes_other = pl.ds(pl.multiple_of((1 - c) * 768, 768), 768)
    lanes_own = pl.ds(pl.multiple_of(c * 768, 768), 768)
    og_copy = remote(out_grad.at[:, lanes_other], og_x, s_ogs, s_ogr, other)
    og_copy.start()

    for part in range(2):
        turn_in(filt.at[part], fil_t.at[part])
    two = jnp.logical_or(n == 0, n == 3)
    sz = [
        lax.rem(z + 3 * (n == 2).astype(jnp.int32), 8),
        lax.rem(z + 8 + (n == 3).astype(jnp.int32) - (n == 0).astype(jnp.int32), 8),
    ]

    def unit_at(zz):
        return zz - (zz >= 3).astype(jnp.int32) - (zz >= 7).astype(jnp.int32)

    def f_src(k, q):
        return fil_t.at[:, pl.ds(q * 96 + unit_at(sz[k]) * 16, 16), :]

    def filter_hop1(k):
        local(f_src(k, p), f1.at[k, p], s1fr.at[k, p])
        over_p(
            lambda q: remote(
                f_src(k, q), f1.at[k, p], s1fs.at[k, q], s1fr.at[k, p], at(q, z, c)
            ).start()
        )

    filter_hop1(0)
    pl.when(two)(lambda: filter_hop1(1))

    def hop2(r1, r1_sem, dst, ss, rs):
        rounds(0, 16, lambda q: landed(r1.at[q], r1_sem.at[q]))
        core = lax.div(n, 2)
        slot = dst.at[lax.rem(n, 2), hc]

        def send(i):
            u = lax.rem(unit + i, 6)
            zz = u + (u >= 2).astype(jnp.int32) + (u >= 5).astype(jnp.int32)
            src = r1.at[:, pl.ds(u * 16, 16), :]
            mine = jnp.logical_and(zz == z, core == c)
            sem = rs.at[lax.rem(n, 2), hc]

            @pl.when(mine)
            def _():
                local(src, slot, sem)

            @pl.when(jnp.logical_not(mine))
            def _():
                remote(src, slot, ss.at[u], sem, at(p, zz, core)).start()

        rounds(0, 6, send)

    def hop2_done(r1, ss):
        core = lax.div(n, 2)

        def done(u):
            zz = u + (u >= 2).astype(jnp.int32) + (u >= 5).astype(jnp.int32)
            mine = jnp.logical_and(zz == z, core == c)

            @pl.when(jnp.logical_not(mine))
            def _():
                left(r1.at[:, pl.ds(u * 16, 16), :], ss.at[u])

        rounds(0, 6, done)

    hop2(r1v, s1vr, xv, s2vs, s2vr)

    def filter_hop2(k):
        rounds(0, 16, lambda q: landed(f1.at[k, q], s1fr.at[k, q]))
        mine = sz[k] == z

        @pl.when(mine)
        def _():
            local(f1.at[k], hx.at[h, c], s2fr.at[h])

        @pl.when(jnp.logical_not(mine))
        def _():
            remote(f1.at[k], hx.at[h, c], s2fs.at[k], s2fr.at[h], at(p, sz[k], c)).start()

    def filter_hop2_done(k):
        @pl.when(sz[k] != z)
        def _():
            left(f1.at[k], s2fs.at[k])

    filter_hop2(0)
    pl.when(two)(lambda: filter_hop2(1))

    turn_in(queries, qt)
    weight_copy.wait()

    def gated_rows(i):
        rows = pl.ds(pl.multiple_of(i * 256, 256), 256)
        g = dot_t(w_in[rows, :], out_grad[...])
        g_gated[rows, :] = g
        gm_t[rows, :] = (g * qt[rows, :].astype(F32)).astype(BF16)

    rounds(0, 6, gated_rows)
    hop1(gm_t, r1g, s1gs, s1gr)

    def transform(src, spec):
        def one(nn):
            def get(hh, cc, yy, xx):
                return src[nn, 2 * hh + cc, 4 * yy + xx].astype(F32)

            def put(s, v):
                co, si = twist[0, s : s + 1, :], twist[1, s : s + 1, :]
                re, im = v
                if im is None:
                    out = (re * co, -(re * si))
                else:
                    out = (re * co + im * si, im * co - re * si)
                for j in range(2):
                    hi, lo = split(out[j])
                    lhi[s * 16 : s * 16 + 16, j * 128 : j * 128 + 128] = hi
                    llo[s * 16 : s * 16 + 16, j * 128 : j * 128 + 128] = lo

            blocks_forward(get, put)
            spec[nn] = dot3(lhi[...], llo[...], m_fwd)

        rounds(0, 2, one)

    def untransform(product, dst):
        def one(nn):
            re, im = product(nn)
            for j, v in enumerate((re, im)):
                hi, lo = split(v)
                lhi[:, j * 128 : j * 128 + 128] = hi
                llo[:, j * 128 : j * 128 + 128] = lo
            back[...] = dot3(lhi[...], llo[...], m_inv)

            def get(s):
                co = twist[0, s : s + 1, :] * (1.0 / SEQ)
                si = twist[1, s : s + 1, :] * (1.0 / SEQ)
                re = back[s * 16 : s * 16 + 16, :128]
                im = back[s * 16 : s * 16 + 16, 128:]
                return (re * co - im * si, im * co + re * si)

            def put(hh, cc, yy, xx, v):
                dst[nn, 2 * hh + cc, 4 * yy + xx] = v.astype(BF16)

            blocks_inverse(get, put)

        rounds(0, 2, one)

    def hop_a(src, dst, ss, rs):
        def send(i):
            nn, hh, cc = lax.div(i, 4), lax.rem(lax.div(i, 2), 2), lax.rem(i, 2)
            zz = hh * 4 + 2 * c + nn
            mine = jnp.logical_and(zz == z, cc == c)

            @pl.when(mine)
            def _():
                local(src.at[nn, 2 * hh + cc], dst.at[unit], rs.at[unit])

            @pl.when(jnp.logical_not(mine))
            def _():
                remote(
                    src.at[nn, 2 * hh + cc], dst.at[unit], ss.at[i], rs.at[unit], at(p, zz, cc)
                ).start()

        rounds(0, 8, send)

    def hop_a_done(src, ss):
        def done(i):
            nn, hh, cc = lax.div(i, 4), lax.rem(lax.div(i, 2), 2), lax.rem(i, 2)
            zz = hh * 4 + 2 * c + nn
            mine = jnp.logical_and(zz == z, cc == c)

            @pl.when(jnp.logical_not(mine))
            def _():
                left(src.at[nn, 2 * hh + cc], ss.at[i])

        rounds(0, 8, done)

    def hop_b(r2, r2_sem, dst, ss, rs):
        rounds(0, 6, lambda u: landed(r2.at[u], r2_sem.at[u]))
        local(r2.at[:, p], dst.at[p], rs.at[p])
        over_p(
            lambda q: remote(r2.at[:, q], dst.at[p], ss.at[q], rs.at[p], at(q, z, c)).start()
        )

    def hop_b_done(r2, ss):
        over_p(lambda q: left(r2.at[:, q], ss.at[q]))

    ident = (
        lax.broadcasted_iota(jnp.int32, (128, 128), 0)
        == lax.broadcasted_iota(jnp.int32, (128, 128), 1)
    ).astype(F32).astype(BF16)
    flip = (
        lax.broadcasted_iota(jnp.int32, (128, 128), 0)
        == 127 - lax.broadcasted_iota(jnp.int32, (128, 128), 1)
    ).astype(F32).astype(BF16)

    @pl.when(active)
    def _():
        for hh in range(2):
            landed(hx.at[hh, c], s2fr.at[hh])
            remote(hx.at[hh, c], hx.at[hh, c], s3fs.at[hh], s3fr.at[hh], other).start()
        rounds(0, 8, lambda i: landed(xv.at[lax.div(i, 4), lax.rem(i, 4)],
                                      s2vr.at[lax.div(i, 4), lax.rem(i, 4)]))
        transform(xv, spec_v)

    hop2(r1g, s1gr, xg, s2gs, s2gr)

    @pl.when(active)
    def _():
        for hh in range(2):
            landed(hx.at[hh, 1 - c], s3fr.at[hh])

        def raw(k):
            return hx[(k >> 3) & 1, k & 1, (k >> 4) * 4 + ((k >> 1) & 3)]

        for k in HELD:
            s = slot_of(k)
            if k % 32:
                hrev[s * 32 : s * 32 + 32, :] = raw(64 - k).reshape(32, 128)
            else:
                hrev[s * 32 : s * 32 + 32, :] = jnp.zeros((32, 128), BF16)
        turned = dot(hrev[...], flip).reshape(SLOTS, 32, 128)
        for k in HELD:
            s = slot_of(k)
            v = raw(k).astype(F32)
            hs[s * 16 : s * 16 + 16, :128] = v[0] + turned[s, :16]
            hs[s * 16 : s * 16 + 16, 128:] = v[1] - turned[s, 16:]

        def mixed_product(nn):
            hr, hi = hs[:, :128], hs[:, 128:]
            vr, vi = spec_v[nn, :, :128], spec_v[nn, :, 128:]
            return hr * vr - hi * vi, hr * vi + hi * vr

        untransform(mixed_product, ymix)
        hop_a(ymix, r2m, sams, samr)
        rounds(0, 8, lambda i: landed(xg.at[lax.div(i, 4), lax.rem(i, 4)],
                                      s2gr.at[lax.div(i, 4), lax.rem(i, 4)]))
        transform(xg, spec_g)

        def value_product(nn):
            hr, hi = hs[:, :128], hs[:, 128:]
            gr_, gi = spec_g[nn, :, :128], spec_g[nn, :, 128:]
            return gr_ * hr + gi * hi, gi * hr - gr_ * hi

        untransform(value_product, ygv)
        hop_a(ygv, r2v, savs, savr)

        re, im = 0.0, 0.0
        for nn in range(2):
            vr, vi = spec_v[nn, :, :128], spec_v[nn, :, 128:]
            gr_, gi = spec_g[nn, :, :128], spec_g[nn, :, 128:]
            re = re + (gr_ * vr + gi * vi)
            im = im + (gi * vr - gr_ * vi)
        gp[:, :128] = re * (1.0 / SEQ)
        gp[:, 128:] = im * (1.0 / SEQ)
        gp_rows = pl.ds(pl.multiple_of((1 - c) * 256, 256), 272)
        remote(gp.at[gp_rows], gpx, s_gps, s_gpr, other).start()

    hop_b(r2m, samr, mix_t, sbms, sbmr)

    @pl.when(active)
    def _():
        landed(gpx, s_gpr)

        def fill(i):
            q, hh = lax.div(i, 2), lax.rem(i, 2)
            a = lax.div(q, 4) * 16 + hh * 8 + lax.rem(q, 4) * 2 + c
            low = lax.rem(a, 4)
            straight = jnp.logical_or(low == 1, jnp.logical_and(c == 0, a <= 32))
            k = jnp.where(straight, a, 64 - a)
            base = jnp.where(lax.rem(k, 4) == 1, 17, jnp.where(lax.rem(k, 4) == 2, 8, 0))
            s = jnp.where(k == 32, 16, base + lax.div(k, 4))
            total = gp[pl.ds(pl.multiple_of(s * 16, 16), 16), :] + gpx[
                pl.ds(pl.multiple_of(s * 16 - 256 * c, 16), 16), :
            ]
            gs[q, hh, 0] = total[:, :128].astype(BF16)
            gs[q, hh, 1] = total[:, 128:].astype(BF16)

        rounds(0, 32, fill)
        local(gs.at[p], gr.at[p], sagr.at[p])
        over_p(
            lambda q: remote(gs.at[q], gr.at[p], sags.at[q], sagr.at[p], at(q, z, c)).start()
        )

    rounds(0, 16, lambda q: landed(mix_t.at[q], sbmr.at[q]))
    mixed = mix_t[...].reshape(D, TOK).astype(F32)
    gat[...] = (qt[...].astype(F32) * mixed).astype(BF16)
    gat_copy = remote(gat, gat_x, s_gts, s_gtr, other)
    gat_copy.start()
    gq = (g_gated[...] * mixed).astype(BF16)
    o_query[...] = dot_t(ident, gq).astype(BF16)

    og_copy.wait_recv()
    gat_copy.wait_recv()

    def weight_rows(i):
        yy, hh = lax.div(i, 2), lax.rem(i, 2)
        rows = pl.ds(pl.multiple_of(i * 192, 192), 192)
        w = dot(gat[rows, :], out_grad[:, lanes_own]) + dot(gat_x[rows, :], og_x[...])
        for part in range(2):
            wa[part, yy, hh] = (
                w[:, part * 384 : (part + 1) * 384].astype(BF16).reshape(4, 48, 384)
            )

    rounds(0, 8, weight_rows)

    def ra_send(i):
        xx, yy = lax.rem(x + i, 4), lax.rem(y + i, 4)
        remote(wa.at[0, :, :, xx], ra0.at[x], sras.at[0, i], srar.at[0, x],
               at(y * 4 + xx, z, c)).start()
        remote(wa.at[1, yy], ra1.at[y], sras.at[1, i], srar.at[1, y],
               at(yy * 4 + x, z, c)).start()

    rounds(1, 4, ra_send)

    hop_b(r2v, savr, gv_t, sbvs, sbvr)

    @pl.when(active)
    def _():
        rounds(0, 16, lambda q: landed(gr.at[q], sagr.at[q]))

        def send(i):
            hh, nn = lax.rem(i, 2), lax.rem(lax.div(i, 2) + n, 4)
            zz = hh * 4 + nn
            sem = sbgr.at[unit]

            @pl.when(zz == z)
            def _():
                local(gr.at[:, hh], gfi.at[:, unit], sem)

            @pl.when(zz != z)
            def _():
                remote(gr.at[:, hh], gfi.at[:, unit], sbgs.at[zz], sem, at(p, zz, c)).start()

        rounds(0, 8, send)

    def ra_wait(i):
        xx, yy = lax.rem(x + i, 4), lax.rem(y + i, 4)
        landed(ra0.at[xx], srar.at[0, xx])
        landed(ra1.at[yy], srar.at[1, yy])

    rounds(1, 4, ra_wait)
    sum0 = wa[0, :, :, x].astype(F32)
    sum1 = wa[1, y].astype(F32)
    for i in range(1, 4):
        sum0 = sum0 + ra0[lax.rem(x + i, 4)].astype(F32)
        sum1 = sum1 + ra1[lax.rem(y + i, 4)].astype(F32)
    sb0[...] = sum0.astype(BF16)
    sb1[...] = sum1.astype(BF16)

    def rb_send(i):
        xx, yy = lax.rem(x + i, 4), lax.rem(y + i, 4)
        remote(sb0.at[yy], rb0.at[y], srbs.at[0, i], srbr.at[0, y], at(yy * 4 + x, z, c)).start()
        remote(sb1.at[:, xx], rb1.at[x], srbs.at[1, i], srbr.at[1, x],
               at(y * 4 + xx, z, c)).start()

    rounds(1, 4, rb_send)

    rounds(0, 16, lambda q: landed(gv_t.at[q], sbvr.at[q]))
    o_value[...] = dot_t(ident, gv_t[...].reshape(D, TOK)).astype(BF16)

    def rb_wait(i):
        xx, yy = lax.rem(x + i, 4), lax.rem(y + i, 4)
        landed(rb0.at[yy], srbr.at[0, yy])
        landed(rb1.at[xx], srbr.at[1, xx])

    rounds(1, 4, rb_wait)
    sum0 = sb0[y].astype(F32)
    sum1 = sb1[:, x].astype(F32)
    for i in range(1, 4):
        sum0 = sum0 + rb0[lax.rem(y + i, 4)].astype(F32)
        sum1 = sum1 + rb1[lax.rem(x + i, 4)].astype(F32)
    sc[:, :, :, :384] = sum0.astype(BF16).reshape(2, 3, 16, 384)
    sc[:, :, :, 384:] = sum1.astype(BF16).reshape(2, 3, 16, 384)

    def rc_send(i):
        hh, t = lax.div(i, 3), lax.rem(i, 3)
        zz = hh * 4 + t

        @pl.when(zz == z)
        def _():
            local(sc.at[hh, t], rc.at[z], srcr.at[z])

        @pl.when(zz != z)
        def _():
            remote(sc.at[hh, t], rc.at[z], srcs.at[i], srcr.at[z], at(p, zz, c)).start()

    rounds(0, 6, rc_send)
    owner = n < 3

    @pl.when(owner)
    def _():
        rounds(0, 8, lambda i: landed(rc.at[i], srcr.at[i]))
        total = rc[0].astype(F32)
        for i in range(1, 8):
            total = total + rc[i].astype(F32)
        sd[...] = total.astype(BF16)

        def send(i):
            nn, cc = lax.div(i, 2), lax.rem(i, 2)
            mine = jnp.logical_and(nn == n, cc == c)

            @pl.when(mine)
            def _():
                local(sd, rd.at[n, c], srdr.at[n, c])

            @pl.when(jnp.logical_not(mine))
            def _():
                remote(sd, rd.at[n, c], srds.at[i], srdr.at[n, c],
                       at(p, h * 4 + nn, cc)).start()

        rounds(0, 8, send)

    def gf_wait(u):
        landed(gfi.at[:, u], sbgr.at[u])

    rounds(0, 6, gf_wait)
    straight = jnp.logical_or(
        lax.rem(ctx, 4) == 1, jnp.logical_and(c == 0, ctx <= 32)
    )
    pick = jnp.where(straight, ident.astype(F32), flip.astype(F32)).astype(BF16)
    sign = jnp.where(straight, 1.0, -1.0)
    o_filter[0] = dot_t(pick, gfi[:, :, 0].reshape(D, TOK))
    o_filter[1] = dot_t(pick, gfi[:, :, 1].reshape(D, TOK)) * sign

    for t in range(3):
        for cc in range(2):
            landed(rd.at[t, cc], srdr.at[t, cc])
    scale = 1.0 / math.sqrt(4 * SEQ)
    for cc in range(2):
        cols = slice(cc * 768, (cc + 1) * 768)

        @pl.when(c == 0)
        def _():
            o_weight[0:16, cols] = rd[0, cc].astype(F32) * scale
            o_weight[16:24, cols] = rd[1, cc].astype(F32)[0:8] * scale

        @pl.when(c == 1)
        def _():
            o_weight[0:8, cols] = rd[1, cc].astype(F32)[8:16] * scale
            o_weight[8:24, cols] = rd[2, cc].astype(F32) * scale

    hop1_done(val_t, s1vs)
    hop1_done(gm_t, s1gs)
    og_copy.wait_send()
    gat_copy.wait_send()
    over_p(lambda q: left(f_src(0, q), s1fs.at[0, q]))
    filter_hop2_done(0)

    @pl.when(two)
    def _():
        over_p(lambda q: left(f_src(1, q), s1fs.at[1, q]))
        filter_hop2_done(1)

    hop2_done(r1v, s2vs)
    hop2_done(r1g, s2gs)
    hop_b_done(r2m, sbms)
    hop_b_done(r2v, sbvs)

    @pl.when(active)
    def _():
        for hh in range(2):
            left(hx.at[hh, c], s3fs.at[hh])
        hop_a_done(ymix, sams)
        hop_a_done(ygv, savs)
        left(gpx, s_gps)
        over_p(lambda q: left(gs.at[q], sags.at[q]))

        def done(zz):
            @pl.when(zz != z)
            def _():
                left(gr.at[:, 0], sbgs.at[zz])

        rounds(0, 8, done)

    def ra_done(i):
        left(ra0.at[0], sras.at[0, i])
        left(ra1.at[0], sras.at[1, i])
        left(rb0.at[0], srbs.at[0, i])
        left(rb1.at[0], srbs.at[1, i])

    rounds(1, 4, ra_done)

    def rc_done(i):
        @pl.when(lax.div(i, 3) * 4 + lax.rem(i, 3) != z)
        def _():
            left(sd, srcs.at[i])

    rounds(0, 6, rc_done)

    @pl.when(owner)
    def _():
        def done(i):
            mine = jnp.logical_and(lax.div(i, 2) == n, lax.rem(i, 2) == c)

            @pl.when(jnp.logical_not(mine))
            def _():
                left(sd, srds.at[i])

        rounds(0, 8, done)


def on_device(queries, values, out_grad, out_weight, filter_spec):
    m_fwd, m_inv, twist = tables()
    vmem = pl.BlockSpec(memory_space=pltpu.VMEM)
    dma = pltpu.SemaphoreType.DMA

    def held(*shape, dtype=BF16):
        return pltpu.VMEM(shape, dtype)

    scratch = [
        held(D, D), held(TOK, 768), held(D, TOK, dtype=F32), held(D, TOK),
        held(D, TOK), held(D, TOK), held(2, D, TOK),
        held(16, 96, TOK), held(16, 96, TOK), held(2, 16, 2, 16, TOK),
        held(2, 4, 16, 16, TOK), held(2, 4, 16, 16, TOK), held(2, 2, 16, 2, 16, TOK),
        held(SLOTS * 32, TOK), held(ROWS, 256, dtype=F32),
        held(ROWS, 256), held(ROWS, 256),
        held(2, ROWS, 256, dtype=F32), held(2, ROWS, 256, dtype=F32), held(ROWS, 256, dtype=F32),
        held(2, 4, 16, 16, TOK), held(2, 4, 16, 16, TOK),
        held(6, 16, 16, TOK), held(6, 16, 16, TOK),
        held(16, 6, 16, TOK), held(16, 6, 16, TOK),
        held(ROWS, 256, dtype=F32), held(272, 256, dtype=F32),
        held(16, 2, 2, 16, TOK), held(16, 2, 2, 16, TOK), held(16, 6, 2, 16, TOK),
        held(D, TOK), held(D, TOK),
        held(2, 4, 2, 4, 48, 384), held(4, 4, 2, 48, 384), held(4, 2, 4, 48, 384),
        held(4, 2, 48, 384), held(2, 4, 48, 384), held(4, 2, 48, 384), held(4, 2, 48, 384),
        held(2, 3, 16, 768), held(8, 16, 768), held(16, 768), held(3, 2, 16, 768),
        dma, dma, dma, dma, dma, dma, dma,
        dma((16,)), dma((16,)), dma((16,)), dma((16,)), dma((2, 16)), dma((2, 16)),
        dma((6,)), dma((2, 4)), dma((6,)), dma((2, 4)), dma((2,)), dma((2,)), dma((2,)), dma((2,)),
        dma((8,)), dma((6,)), dma((8,)), dma((6,)), dma((16,)), dma((16,)), dma((16,)), dma((16,)),
        dma((16,)), dma((16,)), dma((8,)), dma((6,)),
        dma((2, 4)), dma((2, 4)), dma((2, 4)), dma((2, 4)), dma((6,)), dma((8,)),
        dma((8,)), dma((3, 2)),
    ]
    grad_query, grad_value, grad_filter, grad_weight = pl.pallas_call(
        kernel,
        out_shape=(
            jax.ShapeDtypeStruct((TOK, D), BF16),
            jax.ShapeDtypeStruct((TOK, D), BF16),
            jax.ShapeDtypeStruct((2, TOK, D), F32),
            jax.ShapeDtypeStruct((24, D), F32),
        ),
        in_specs=[vmem, vmem, vmem, pl.BlockSpec(memory_space=pl.ANY)] + [vmem] * 4,
        out_specs=(vmem,) * 4,
        scratch_shapes=scratch,
        compiler_params=pltpu.CompilerParams(
            collective_id=0, has_side_effects=True, vmem_limit_bytes=52 * 2**20
        ),
    )(values[0], queries[0], out_grad[0], out_weight, filter_spec,
      jnp.asarray(m_fwd), jnp.asarray(m_inv), jnp.asarray(twist))
    return grad_query[None], grad_value[None], grad_filter, grad_weight


def solution(mesh):
    return jax.shard_map(
        on_device,
        mesh=mesh,
        in_specs=(
            P("dp", "ctx", None),
            P("dp", "ctx", None),
            P("dp", "ctx", None),
            P(),
            P(None, "ctx", None),
        ),
        out_specs=(
            P("dp", "ctx", None),
            P("dp", "ctx", None),
            P(None, "ctx", None),
            P("ctx", None),
        ),
        check_vma=False,
    )
```

```python
import functools
import math

import jax
import jax.numpy as jnp
import numpy as np
from jax import lax
from jax.experimental import pallas as pl
from jax.experimental.pallas import tpu as pltpu
from jax.sharding import PartitionSpec as P

F32 = jnp.float32
BF16 = jnp.bfloat16
TOK = 128
D = 1536
SEQ = 8192
SLOTS = 33
ROWS = SLOTS * 16
MESH = pl.DeviceIdType.MESH


def slot_of(k):
    if k == 32:
        return 16
    if k % 4 == 0:
        return k // 4
    if k % 4 == 2:
        return 8 + k // 4
    return 17 + k // 4


HELD = [k for k in range(64) if k % 4 == 1 or (k % 2 == 0 and k <= 32)]


def tables():
    r = np.arange(TOK)
    angle = 2.0 * math.pi * ((r[:, None] * r[None, :]) % TOK) / TOK
    c, s = np.cos(angle), np.sin(angle)
    forward = np.block([[c, -s], [s, c]])
    inverse = np.block([[c, s], [-s, c]])

    def halves(m):
        hi = m.astype(np.float32).astype(jnp.bfloat16)
        lo = (m - hi.astype(np.float64)).astype(np.float32).astype(jnp.bfloat16)
        return np.stack([hi, lo])

    twist = np.zeros((2, 40, TOK), np.float32)
    for k in HELD:
        a = 2.0 * math.pi * k * r / SEQ
        twist[0, slot_of(k)] = np.cos(a)
        twist[1, slot_of(k)] = np.sin(a)
    return halves(forward), halves(inverse), twist


def p_add(a, b):
    if a is None:
        return b
    return a if b is None else a + b


def p_sub(a, b):
    if b is None:
        return a
    return -b if a is None else a - b


def c_add(a, b):
    return (p_add(a[0], b[0]), p_add(a[1], b[1]))


def c_sub(a, b):
    return (p_sub(a[0], b[0]), p_sub(a[1], b[1]))


def by_i(a):
    return (p_sub(None, a[1]), a[0])


def p_mul(a, f):
    return None if a is None or f == 0.0 else a * f


def turn(z, k, n):
    k = k % n
    if k == 0:
        return z
    if 4 * k == n:
        return by_i(z)
    if 2 * k == n:
        return c_sub((None, None), z)
    if 4 * k == 3 * n:
        return (z[1], p_sub(None, z[0]))
    c, s = math.cos(2 * math.pi * k / n), math.sin(2 * math.pi * k / n)
    return (
        p_sub(p_mul(z[0], c), p_mul(z[1], s)),
        p_add(p_mul(z[0], s), p_mul(z[1], c)),
    )


def four(z, sign):
    t0, t1 = c_add(z[0], z[2]), c_sub(z[0], z[2])
    t2, t3 = c_add(z[1], z[3]), by_i(c_sub(z[1], z[3]))
    if sign < 0:
        return [c_add(t0, t2), c_sub(t1, t3), c_sub(t0, t2), c_add(t1, t3)]
    return [c_add(t0, t2), c_add(t1, t3), c_sub(t0, t2), c_sub(t1, t3)]


def blocks_forward(get, put):
    t = {}
    for h in range(2):
        for c in range(2):
            for x in range(4):
                v = [get(h, c, y, x) for y in range(4)]
                s02, d02 = v[0] + v[2], v[0] - v[2]
                s13, d13 = v[1] + v[3], v[1] - v[3]
                a = 8 * h + 2 * x + c
                t[0, h, c, x] = (s02 + s13, None)
                t[1, h, c, x] = turn((d02, -d13), -a, 64)
                t[2, h, c, x] = turn((s02 - s13, None), -2 * a, 64)
    for ky in range(3):
        for kh in range(2):
            halves = []
            for c in range(2):
                z = []
                for x in range(4):
                    if kh == 0:
                        z.append(c_add(t[ky, 0, c, x], t[ky, 1, c, x]))
                    else:
                        z.append(turn(c_sub(t[ky, 0, c, x], t[ky, 1, c, x]), -(2 * x + c), 16))
                z = four(z, -1)
                if c == 1:
                    z = [turn(z[kx], -kx, 8) for kx in range(4)]
                halves.append(z)
            for kx in range(4):
                k = ky + 4 * kh + 8 * kx
                put(slot_of(k), c_add(halves[0][kx], halves[1][kx]))
                if ky == 1 or k == 0:
                    put(slot_of(k + 32), c_sub(halves[0][kx], halves[1][kx]))


def blocks_inverse(get, put):
    u = {}
    for ky in range(3):
        for kh in range(2):
            lanes = [[], []]
            for kx in range(4):
                k = ky + 4 * kh + 8 * kx
                z = get(slot_of(k))
                if ky == 1 or k == 0:
                    w = get(slot_of(k + 32))
                    first, second = c_add(z, w), c_sub(z, w)
                else:
                    first, second = z, z
                lanes[0].append(first)
                lanes[1].append(turn(second, kx, 8))
            for c in range(2):
                z = four(lanes[c], 1)
                for x in range(4):
                    u[ky, kh, c, x] = turn(z[x], (2 * x + c) * kh, 16)
    for c in range(2):
        for x in range(4):
            for h in range(2):
                a = 8 * h + 2 * x + c
                join = c_add if h == 0 else c_sub
                u0 = join(u[0, 0, c, x], u[0, 1, c, x])[0]
                u1 = turn(join(u[1, 0, c, x], u[1, 1, c, x]), a, 64)
                u2 = turn(join(u[2, 0, c, x], u[2, 1, c, x]), 2 * a, 64)[0]
                even, odd = u0 + u2, u0 - u2
                put(h, c, 0, x, even + u1[0])
                put(h, c, 1, x, odd - u1[1])
                put(h, c, 2, x, even - u1[0])
                put(h, c, 3, x, odd + u1[1])


def split(v):
    hi = v.astype(BF16)
    return hi, (v - hi.astype(F32)).astype(BF16)


def dot(a, b):
    return jnp.dot(a, b, preferred_element_type=F32)


def dot_t(a, b):
    return lax.dot_general(a, b, (((1,), (1,)), ((), ())), preferred_element_type=F32)


def dot3(hi, lo, m):
    return dot(hi, m[0]) + dot(lo, m[0]) + dot(hi, m[1])


def kernel(
    h_values, h_queries, h_out_grad, h_weight, h_filt, h_fwd, h_inv, h_twist,
    o_query, o_value, o_filter, o_weight,
    values, queries, out_grad, w_in, filt, m_fwd, m_inv, twist,
    g_gated, qt, val_t, gm_t, fil_t,
    r1v, r1g, f1, xv, xg, hx, hrev, hs, lhi, llo, spec_v, spec_g, back,
    ymix, ygv, r2m, r2v, mix_t, gv_t, gp, gpx, gs, gr, gfi,
    gat, og_all, gat_all, wb, ry, sc, rc, sd, rd,
    s_in, s_ogs, s_ogr, s_gas, s_gar, s_gxs, s_gps, s_gpr,
    s1vs, s1vr, s1gs, s1gr, s1fs, s1fr,
    s2vs, s2vr, s2gs, s2gr, s2fs, s2fr, s3fs, s3fr,
    sams, samr, savs, savr, sbms, sbmr, sbvs, sbvr,
    sags, sagr, sbgs, sbgr,
    srys, sryr, srcs, srcr, srds, srdr,
):
    n = lax.axis_index("dp")
    ctx = lax.axis_index("ctx")
    y, h = lax.div(ctx, 16), lax.rem(lax.div(ctx, 8), 2)
    x, c = lax.rem(lax.div(ctx, 2), 4), lax.rem(ctx, 2)
    p, z = y * 4 + x, h * 4 + n
    hc = h * 2 + c
    active = n != 2
    unit = z - (z >= 3).astype(jnp.int32) - (z >= 7).astype(jnp.int32)

    def at(pp, zz, cc):
        return (
            lax.rem(zz, 4),
            lax.div(pp, 4) * 16 + lax.div(zz, 4) * 8 + lax.rem(pp, 4) * 2 + cc,
        )

    def remote(src, dst, ss, rs, dev):
        return pltpu.make_async_remote_copy(
            src_ref=src, dst_ref=dst, send_sem=ss, recv_sem=rs,
            device_id=dev, device_id_type=MESH,
        )

    def local(src, dst, sem):
        pltpu.make_async_copy(src, dst, sem).start()

    def landed(dst, sem):
        pltpu.make_async_copy(dst, dst, sem).wait()

    def left(src, sem):
        pltpu.make_async_copy(src, src, sem).wait()

    def rounds(lo, hi, body):
        lax.fori_loop(lo, hi, lambda i, carry: (body(i), carry)[1], 0)

    def place(i):
        return lax.rem(y + lax.div(i, 4), 4) * 4 + lax.rem(x + lax.rem(i, 4), 4)

    def over_p(send):
        rounds(1, 16, lambda i: send(place(i)))

    inputs = [
        pltpu.make_async_copy(src, dst, s_in.at[i])
        for i, (src, dst) in enumerate(
            [
                (h_values, values), (h_queries, queries), (h_out_grad, out_grad),
                (h_weight, w_in), (h_filt, filt), (h_fwd, m_fwd), (h_inv, m_inv),
                (h_twist, twist),
            ]
        )
    ]
    for copy in inputs:
        copy.start()

    barrier = pltpu.get_barrier_semaphore()

    def greet(dev):
        pl.semaphore_signal(barrier, inc=1, device_id=dev, device_id_type=MESH)

    over_p(lambda q: greet(at(q, z, c)))
    rounds(
        1, 16,
        lambda i: greet(
            at(p, lax.rem(z + lax.div(i, 2), 8), lax.rem(c + lax.rem(i, 2), 2))
        ),
    )
    rounds(1, 4, lambda i: greet(at(y * 4 + lax.rem(x + i, 4), z, 1 - c)))

    def turn_in(src, dst):
        for j in range(D // 128):
            dst[j * 128 : (j + 1) * 128, :] = src[:, j * 128 : (j + 1) * 128].T

    inputs[0].wait()
    turn_in(values, val_t)
    pl.semaphore_wait(barrier, 33)

    def hop1(src, dst, ss, rs):
        local(src.at[pl.ds(p * 96, 96)], dst.at[p], rs.at[p])
        over_p(
            lambda q: remote(
                src.at[pl.ds(q * 96, 96)], dst.at[p], ss.at[q], rs.at[p], at(q, z, c)
            ).start()
        )

    def hop1_done(src, ss):
        over_p(lambda q: left(src.at[pl.ds(q * 96, 96)], ss.at[q]))

    hop1(val_t, r1v, s1vs, s1vr)

    inputs[1].wait()
    turn_in(queries, qt)
    inputs[2].wait()
    inputs[3].wait()

    def gated_rows(i):
        rows = pl.ds(pl.multiple_of(i * 256, 256), 256)
        g = dot_t(w_in[rows, :], out_grad[...])
        g_gated[rows, :] = g
        gm_t[rows, :] = (g * qt[rows, :].astype(F32)).astype(BF16)

    rounds(0, 6, gated_rows)

    inputs[4].wait()
    for part in range(2):
        turn_in(filt.at[part], fil_t.at[part])
    two = jnp.logical_or(n == 0, n == 3)
    sz = [
        lax.rem(z + 3 * (n == 2).astype(jnp.int32), 8),
        lax.rem(z + 8 + (n == 3).astype(jnp.int32) - (n == 0).astype(jnp.int32), 8),
    ]

    def unit_at(zz):
        return zz - (zz >= 3).astype(jnp.int32) - (zz >= 7).astype(jnp.int32)

    def f_src(k, q):
        return fil_t.at[:, pl.ds(q * 96 + unit_at(sz[k]) * 16, 16), :]

    def filter_hop1(k):
        local(f_src(k, p), f1.at[k, p], s1fr.at[k, p])
        over_p(
            lambda q: remote(
                f_src(k, q), f1.at[k, p], s1fs.at[k, q], s1fr.at[k, p], at(q, z, c)
            ).start()
        )

    filter_hop1(0)
    pl.when(two)(lambda: filter_hop1(1))
    hop1(gm_t, r1g, s1gs, s1gr)

    core = lax.div(n, 2)

    def z_of(u):
        return u + (u >= 2).astype(jnp.int32) + (u >= 5).astype(jnp.int32)

    def hop2(r1, r1_sem, dst, ss, rs):
        def row(j):
            yy = lax.rem(y + j, 4)
            blocks = pl.ds(yy * 4, 4)
            rounds(0, 4, lambda q: landed(r1.at[yy * 4 + q], r1_sem.at[yy * 4 + q]))
            slot = dst.at[lax.rem(n, 2), hc, blocks]
            sem = rs.at[lax.rem(n, 2), hc]

            def send(i):
                u = lax.rem(unit + i, 6)
                zz = z_of(u)
                src = r1.at[blocks, pl.ds(u * 16, 16), :]
                mine = jnp.logical_and(zz == z, core == c)

                @pl.when(mine)
                def _():
                    local(src, slot, sem)

                @pl.when(jnp.logical_not(mine))
                def _():
                    remote(src, slot, ss.at[u], sem, at(p, zz, core)).start()

            rounds(0, 6, send)

        rounds(0, 4, row)

    def hop2_done(r1, ss):
        def done(u):
            mine = jnp.logical_and(z_of(u) == z, core == c)

            @pl.when(jnp.logical_not(mine))
            def _():
                left(r1.at[:, pl.ds(u * 16, 16), :], ss.at[u])

        rounds(0, 6, done)

    hop2(r1v, s1vr, xv, s2vs, s2vr)

    def filter_hop2(k):
        rounds(0, 16, lambda q: landed(f1.at[k, q], s1fr.at[k, q]))
        mine = sz[k] == z

        @pl.when(mine)
        def _():
            local(f1.at[k], hx.at[h, c], s2fr.at[h])

        @pl.when(jnp.logical_not(mine))
        def _():
            remote(f1.at[k], hx.at[h, c], s2fs.at[k], s2fr.at[h], at(p, sz[k], c)).start()

    def filter_hop2_done(k):
        @pl.when(sz[k] != z)
        def _():
            left(f1.at[k], s2fs.at[k])

    filter_hop2(0)
    pl.when(two)(lambda: filter_hop2(1))
    hop2(r1g, s1gr, xg, s2gs, s2gr)

    other = at(p, z, 1 - c)

    def og_send(i):
        xx, cc = lax.rem(x + lax.div(i, 2), 4), lax.rem(c + lax.rem(i, 2), 2)
        half = pl.ds(pl.multiple_of(cc * 768, 768), 768)
        slot = og_all.at[x, pl.ds(pl.multiple_of(c * 128, 128), 128)]
        remote(
            out_grad.at[:, half], slot, s_ogs.at[i], s_ogr.at[x, c], at(y * 4 + xx, z, cc)
        ).start()

    own_half = pl.ds(pl.multiple_of(c * 768, 768), 768)
    own_depth = pl.ds(pl.multiple_of(c * 128, 128), 128)
    local(out_grad.at[:, own_half], og_all.at[x, own_depth], s_ogr.at[x, c])
    rounds(1, 8, og_send)

    def transform(src, spec, nn):
        def get(hh, cc, yy, xx):
            return src[nn, 2 * hh + cc, 4 * yy + xx].astype(F32)

        def put(s, v):
            co, si = twist[0, s : s + 1, :], twist[1, s : s + 1, :]
            re, im = v
            if im is None:
                out = (re * co, -(re * si))
            else:
                out = (re * co + im * si, im * co - re * si)
            for j in range(2):
                hi, lo = split(out[j])
                lhi[s * 16 : s * 16 + 16, j * 128 : j * 128 + 128] = hi
                llo[s * 16 : s * 16 + 16, j * 128 : j * 128 + 128] = lo

        blocks_forward(get, put)
        spec[nn] = dot3(lhi[...], llo[...], m_fwd)

    def untransform(product, dst, nn):
        for j, v in enumerate(product):
            hi, lo = split(v)
            lhi[:, j * 128 : j * 128 + 128] = hi
            llo[:, j * 128 : j * 128 + 128] = lo
        back[...] = dot3(lhi[...], llo[...], m_inv)

        def get(s):
            co = twist[0, s : s + 1, :] * (1.0 / SEQ)
            si = twist[1, s : s + 1, :] * (1.0 / SEQ)
            re = back[s * 16 : s * 16 + 16, :128]
            im = back[s * 16 : s * 16 + 16, 128:]
            return (re * co - im * si, im * co + re * si)

        def put(hh, cc, yy, xx, v):
            dst[nn, 2 * hh + cc, 4 * yy + xx] = v.astype(BF16)

        blocks_inverse(get, put)

    def hop_a(src, dst, ss, rs, nn):
        def send(j):
            i = nn * 4 + j
            hh, cc = lax.rem(lax.div(i, 2), 2), lax.rem(i, 2)
            zz = hh * 4 + 2 * c + nn
            mine = jnp.logical_and(zz == z, cc == c)

            @pl.when(mine)
            def _():
                local(src.at[nn, 2 * hh + cc], dst.at[unit], rs.at[unit])

            @pl.when(jnp.logical_not(mine))
            def _():
                remote(
                    src.at[nn, 2 * hh + cc], dst.at[unit], ss.at[i], rs.at[unit], at(p, zz, cc)
                ).start()

        rounds(0, 4, send)

    def hop_a_done(src, ss):
        def done(i):
            nn, hh, cc = lax.div(i, 4), lax.rem(lax.div(i, 2), 2), lax.rem(i, 2)
            zz = hh * 4 + 2 * c + nn
            mine = jnp.logical_and(zz == z, cc == c)

            @pl.when(jnp.logical_not(mine))
            def _():
                left(src.at[nn, 2 * hh + cc], ss.at[i])

        rounds(0, 8, done)

    def hop_b(r2, r2_sem, dst, ss, rs):
        def relay(i):
            u = lax.rem(unit + i, 6)
            landed(r2.at[u], r2_sem.at[u])
            local(r2.at[u, p], dst.at[p, u], rs.at[p])
            over_p(
                lambda q: remote(
                    r2.at[u, q], dst.at[p, u], ss.at[q], rs.at[p], at(q, z, c)
                ).start()
            )

        rounds(0, 6, relay)

    def hop_b_done(r2, ss):
        over_p(lambda q: left(r2.at[:, q], ss.at[q]))

    ident = (
        lax.broadcasted_iota(jnp.int32, (128, 128), 0)
        == lax.broadcasted_iota(jnp.int32, (128, 128), 1)
    ).astype(F32).astype(BF16)
    flip = (
        lax.broadcasted_iota(jnp.int32, (128, 128), 0)
        == 127 - lax.broadcasted_iota(jnp.int32, (128, 128), 1)
    ).astype(F32).astype(BF16)

    for copy in inputs[5:]:
        copy.wait()

    @pl.when(active)
    def _():
        for hh in range(2):
            landed(hx.at[hh, c], s2fr.at[hh])
            remote(hx.at[hh, c], hx.at[hh, c], s3fs.at[hh], s3fr.at[hh], other).start()
        for hh in range(2):
            landed(hx.at[hh, 1 - c], s3fr.at[hh])

        def raw(k):
            return hx[(k >> 3) & 1, k & 1, (k >> 4) * 4 + ((k >> 1) & 3)]

        for k in HELD:
            s = slot_of(k)
            if k % 32:
                hrev[s * 32 : s * 32 + 32, :] = raw(64 - k).reshape(32, 128)
            else:
                hrev[s * 32 : s * 32 + 32, :] = jnp.zeros((32, 128), BF16)
        turned = dot(hrev[...], flip).reshape(SLOTS, 32, 128)
        for k in HELD:
            s = slot_of(k)
            v = raw(k).astype(F32)
            hs[s * 16 : s * 16 + 16, :128] = v[0] + turned[s, :16]
            hs[s * 16 : s * 16 + 16, 128:] = v[1] - turned[s, 16:]

        def values_part(nn):
            rounds(0, 4, lambda i: landed(xv.at[nn, i], s2vr.at[nn, i]))
            transform(xv, spec_v, nn)
            hr, hi = hs[:, :128], hs[:, 128:]
            vr, vi = spec_v[nn, :, :128], spec_v[nn, :, 128:]
            untransform((hr * vr - hi * vi, hr * vi + hi * vr), ymix, nn)
            hop_a(ymix, r2m, sams, samr, nn)

        rounds(0, 2, values_part)

        def grads_part(nn):
            rounds(0, 4, lambda i: landed(xg.at[nn, i], s2gr.at[nn, i]))
            transform(xg, spec_g, nn)
            hr, hi = hs[:, :128], hs[:, 128:]
            gr_, gi = spec_g[nn, :, :128], spec_g[nn, :, 128:]
            untransform((gr_ * hr + gi * hi, gi * hr - gr_ * hi), ygv, nn)
            hop_a(ygv, r2v, savs, savr, nn)

        rounds(0, 2, grads_part)
        re, im = 0.0, 0.0
        for nn in range(2):
            vr, vi = spec_v[nn, :, :128], spec_v[nn, :, 128:]
            gr_, gi = spec_g[nn, :, :128], spec_g[nn, :, 128:]
            re = re + (gr_ * vr + gi * vi)
            im = im + (gi * vr - gr_ * vi)
        gp[:, :128] = re * (1.0 / SEQ)
        gp[:, 128:] = im * (1.0 / SEQ)
        gp_rows = pl.ds(pl.multiple_of((1 - c) * 256, 256), 272)
        remote(gp.at[gp_rows], gpx, s_gps, s_gpr, other).start()

    hop_b(r2m, samr, mix_t, sbms, sbmr)

    @pl.when(active)
    def _():
        landed(gpx, s_gpr)

        def fill(i):
            q, hh = lax.div(i, 2), lax.rem(i, 2)
            a = lax.div(q, 4) * 16 + hh * 8 + lax.rem(q, 4) * 2 + c
            low = lax.rem(a, 4)
            straight = jnp.logical_or(low == 1, jnp.logical_and(c == 0, a <= 32))
            k = jnp.where(straight, a, 64 - a)
            base = jnp.where(lax.rem(k, 4) == 1, 17, jnp.where(lax.rem(k, 4) == 2, 8, 0))
            s = jnp.where(k == 32, 16, base + lax.div(k, 4))
            total = gp[pl.ds(pl.multiple_of(s * 16, 16), 16), :] + gpx[
                pl.ds(pl.multiple_of(s * 16 - 256 * c, 16), 16), :
            ]
            gs[q, hh, 0] = total[:, :128].astype(BF16)
            gs[q, hh, 1] = total[:, 128:].astype(BF16)

        rounds(0, 32, fill)
        local(gs.at[p], gr.at[p], sagr.at[p])
        over_p(
            lambda q: remote(gs.at[q], gr.at[p], sags.at[q], sagr.at[p], at(q, z, c)).start()
        )

    rounds(0, 16, lambda q: landed(mix_t.at[q], sbmr.at[q]))
    mixed = mix_t[...].reshape(D, TOK).astype(F32)
    gat[...] = (qt[...].astype(F32) * mixed).astype(BF16).reshape(8, 4, 48, TOK)

    def gat_send(i):
        xx = lax.rem(x + i, 4)
        remote(
            gat.at[:, xx], gat_all.at[x, :, :, own_depth], s_gas.at[i], s_gar.at[x, c],
            at(y * 4 + xx, z, c),
        ).start()

    rounds(1, 4, gat_send)
    local(gat.at[:, x], gat_all.at[x, :, :, own_depth], s_gar.at[x, c])
    @pl.when(active)
    def _():
        rounds(0, 16, lambda q: landed(gr.at[q], sagr.at[q]))

        def send(i):
            hh, nn = lax.rem(i, 2), lax.rem(lax.div(i, 2) + n, 4)
            zz = hh * 4 + nn
            sem = sbgr.at[unit]

            @pl.when(zz == z)
            def _():
                local(gr.at[:, hh], gfi.at[:, unit], sem)

            @pl.when(zz != z)
            def _():
                remote(gr.at[:, hh], gfi.at[:, unit], sbgs.at[zz], sem, at(p, zz, c)).start()

        rounds(0, 8, send)

    gq = (g_gated[...] * mixed).astype(BF16)
    o_query[...] = dot_t(ident, gq).astype(BF16)

    def gat_pass(i):
        xx = lax.rem(x + i, 4)
        here = gat_all.at[xx, :, :, own_depth]
        landed(here, s_gar.at[xx, c])
        remote(here, here, s_gxs.at[xx], s_gar.at[xx, c], other).start()

    rounds(0, 4, gat_pass)

    other_depth = pl.ds(pl.multiple_of((1 - c) * 128, 128), 128)

    def w_wait(xx):
        landed(gat_all.at[xx, :, :, other_depth], s_gar.at[xx, 1 - c])
        landed(og_all.at[xx, own_depth], s_ogr.at[xx, c])
        landed(og_all.at[xx, other_depth], s_ogr.at[xx, 1 - c])

    rounds(0, 4, w_wait)

    def weight_rows(i):
        yy = lax.rem(y + i, 4)
        total = dot(gat_all[0, pl.ds(yy * 2, 2)].reshape(96, 256), og_all[0])
        for xx in range(1, 4):
            total = total + dot(gat_all[xx, pl.ds(yy * 2, 2)].reshape(96, 256), og_all[xx])
        wb[yy] = total.astype(BF16).reshape(2, 48, 768)

        @pl.when(i < 4)
        def _():
            remote(wb.at[yy], ry.at[y], srys.at[i], sryr.at[y], at(yy * 4 + x, z, c)).start()

    rounds(1, 5, weight_rows)
    hop_b(r2v, savr, gv_t, sbvs, sbvr)

    rounds(1, 4, lambda i: landed(ry.at[lax.rem(y + i, 4)], sryr.at[lax.rem(y + i, 4)]))
    total = wb[y].astype(F32)
    for i in range(1, 4):
        total = total + ry[lax.rem(y + i, 4)].astype(F32)
    sc[...] = total.astype(BF16).reshape(2, 3, 16, 768)

    def rc_send(i):
        hh, t = lax.div(i, 3), lax.rem(i, 3)
        zz = hh * 4 + t

        @pl.when(zz == z)
        def _():
            local(sc.at[hh, t], rc.at[z], srcr.at[z])

        @pl.when(zz != z)
        def _():
            remote(sc.at[hh, t], rc.at[z], srcs.at[i], srcr.at[z], at(p, zz, c)).start()

    rounds(0, 6, rc_send)

    rounds(0, 16, lambda q: landed(gv_t.at[q], sbvr.at[q]))
    o_value[...] = dot_t(ident, gv_t[...].reshape(D, TOK)).astype(BF16)
    owner = n < 3

    @pl.when(owner)
    def _():
        rounds(0, 8, lambda i: landed(rc.at[i], srcr.at[i]))
        total = rc[0].astype(F32)
        for i in range(1, 8):
            total = total + rc[i].astype(F32)
        sd[...] = total.astype(BF16)

        def send(i):
            nn, cc = lax.div(i, 2), lax.rem(i, 2)
            mine = jnp.logical_and(nn == n, cc == c)

            @pl.when(mine)
            def _():
                local(sd, rd.at[n, c], srdr.at[n, c])

            @pl.when(jnp.logical_not(mine))
            def _():
                remote(sd, rd.at[n, c], srds.at[i], srdr.at[n, c],
                       at(p, h * 4 + nn, cc)).start()

        rounds(0, 8, send)

    rounds(0, 6, lambda u: landed(gfi.at[:, u], sbgr.at[u]))
    straight = jnp.logical_or(
        lax.rem(ctx, 4) == 1, jnp.logical_and(c == 0, ctx <= 32)
    )
    pick = jnp.where(straight, ident.astype(F32), flip.astype(F32)).astype(BF16)
    sign = jnp.where(straight, 1.0, -1.0)
    o_filter[0] = dot_t(pick, gfi[:, :, 0].reshape(D, TOK))
    o_filter[1] = dot_t(pick, gfi[:, :, 1].reshape(D, TOK)) * sign

    for t in range(3):
        for cc in range(2):
            landed(rd.at[t, cc], srdr.at[t, cc])
    scale = 1.0 / math.sqrt(4 * SEQ)
    for cc in range(2):
        cols = slice(cc * 768, (cc + 1) * 768)

        @pl.when(c == 0)
        def _():
            o_weight[0:16, cols] = rd[0, cc].astype(F32) * scale
            o_weight[16:24, cols] = rd[1, cc].astype(F32)[0:8] * scale

        @pl.when(c == 1)
        def _():
            o_weight[0:8, cols] = rd[1, cc].astype(F32)[8:16] * scale
            o_weight[8:24, cols] = rd[2, cc].astype(F32) * scale

    hop1_done(val_t, s1vs)
    hop1_done(gm_t, s1gs)
    over_p(lambda q: left(f_src(0, q), s1fs.at[0, q]))
    filter_hop2_done(0)

    @pl.when(two)
    def _():
        over_p(lambda q: left(f_src(1, q), s1fs.at[1, q]))
        filter_hop2_done(1)

    hop2_done(r1v, s2vs)
    hop2_done(r1g, s2gs)
    hop_b_done(r2m, sbms)
    hop_b_done(r2v, sbvs)
    rounds(1, 8, lambda i: left(og_all.at[x, own_depth], s_ogs.at[i]))
    rounds(1, 4, lambda i: left(gat.at[:, x], s_gas.at[i]))
    rounds(0, 4, lambda i: left(gat_all.at[i, :, :, own_depth], s_gxs.at[i]))

    @pl.when(active)
    def _():
        for hh in range(2):
            left(hx.at[hh, c], s3fs.at[hh])
        hop_a_done(ymix, sams)
        hop_a_done(ygv, savs)
        left(gpx, s_gps)
        over_p(lambda q: left(gs.at[q], sags.at[q]))

        def done(zz):
            @pl.when(zz != z)
            def _():
                left(gr.at[:, 0], sbgs.at[zz])

        rounds(0, 8, done)

    rounds(1, 4, lambda i: left(wb.at[0], srys.at[i]))

    def rc_done(i):
        @pl.when(lax.div(i, 3) * 4 + lax.rem(i, 3) != z)
        def _():
            left(sd, srcs.at[i])

    rounds(0, 6, rc_done)

    @pl.when(owner)
    def _():
        def done(i):
            mine = jnp.logical_and(lax.div(i, 2) == n, lax.rem(i, 2) == c)

            @pl.when(jnp.logical_not(mine))
            def _():
                left(sd, srds.at[i])

        rounds(0, 8, done)


def on_device(queries, values, out_grad, out_weight, filter_spec):
    m_fwd, m_inv, twist = tables()
    vmem = pl.BlockSpec(memory_space=pltpu.VMEM)
    dma = pltpu.SemaphoreType.DMA

    def held(*shape, dtype=BF16):
        return pltpu.VMEM(shape, dtype)

    scratch = [
        held(TOK, D), held(TOK, D), held(TOK, D), held(D, D), held(2, TOK, D),
        held(2, 256, 256), held(2, 256, 256), held(2, 40, TOK, dtype=F32),
        held(D, TOK, dtype=F32), held(D, TOK), held(D, TOK), held(D, TOK), held(2, D, TOK),
        held(16, 96, TOK), held(16, 96, TOK), held(2, 16, 2, 16, TOK),
        held(2, 4, 16, 16, TOK), held(2, 4, 16, 16, TOK), held(2, 2, 16, 2, 16, TOK),
        held(SLOTS * 32, TOK), held(ROWS, 256, dtype=F32),
        held(ROWS, 256), held(ROWS, 256),
        held(2, ROWS, 256, dtype=F32), held(2, ROWS, 256, dtype=F32), held(ROWS, 256, dtype=F32),
        held(2, 4, 16, 16, TOK), held(2, 4, 16, 16, TOK),
        held(6, 16, 16, TOK), held(6, 16, 16, TOK),
        held(16, 6, 16, TOK), held(16, 6, 16, TOK),
        held(ROWS, 256, dtype=F32), held(272, 256, dtype=F32),
        held(16, 2, 2, 16, TOK), held(16, 2, 2, 16, TOK), held(16, 6, 2, 16, TOK),
        held(8, 4, 48, TOK), held(4, 256, 768), held(4, 8, 48, 256),
        held(4, 2, 48, 768), held(4, 2, 48, 768),
        held(2, 3, 16, 768), held(8, 16, 768), held(16, 768), held(3, 2, 16, 768),
        dma((8,)), dma((8,)), dma((4, 2)), dma((4,)), dma((4, 2)), dma((4,)), dma, dma,
        dma((16,)), dma((16,)), dma((16,)), dma((16,)), dma((2, 16)), dma((2, 16)),
        dma((6,)), dma((2, 4)), dma((6,)), dma((2, 4)), dma((2,)), dma((2,)), dma((2,)), dma((2,)),
        dma((8,)), dma((6,)), dma((8,)), dma((6,)), dma((16,)), dma((16,)), dma((16,)), dma((16,)),
        dma((16,)), dma((16,)), dma((8,)), dma((6,)),
        dma((4,)), dma((4,)), dma((6,)), dma((8,)), dma((8,)), dma((3, 2)),
    ]
    grad_query, grad_value, grad_filter, grad_weight = pl.pallas_call(
        kernel,
        out_shape=(
            jax.ShapeDtypeStruct((TOK, D), BF16),
            jax.ShapeDtypeStruct((TOK, D), BF16),
            jax.ShapeDtypeStruct((2, TOK, D), F32),
            jax.ShapeDtypeStruct((24, D), F32),
        ),
        in_specs=[pl.BlockSpec(memory_space=pl.ANY)] * 8,
        out_specs=(vmem,) * 4,
        scratch_shapes=scratch,
        compiler_params=pltpu.CompilerParams(
            collective_id=0, has_side_effects=True, vmem_limit_bytes=60 * 2**20
        ),
    )(values[0], queries[0], out_grad[0], out_weight, filter_spec,
      jnp.asarray(m_fwd), jnp.asarray(m_inv), jnp.asarray(twist))
    return grad_query[None], grad_value[None], grad_filter, grad_weight


def solution(mesh):
    return jax.shard_map(
        on_device,
        mesh=mesh,
        in_specs=(
            P("dp", "ctx", None),
            P("dp", "ctx", None),
            P("dp", "ctx", None),
            P(),
            P(None, "ctx", None),
        ),
        out_specs=(
            P("dp", "ctx", None),
            P("dp", "ctx", None),
            P(None, "ctx", None),
            P("ctx", None),
        ),
        check_vma=False,
    )
```

```python
import functools
import math

import jax
import jax.numpy as jnp
import numpy as np
from jax import lax
from jax.experimental import pallas as pl
from jax.experimental.pallas import tpu as pltpu
from jax.sharding import PartitionSpec as P

F32 = jnp.float32
BF16 = jnp.bfloat16
TOK = 128
D = 1536
SEQ = 8192
SLOTS = 33
ROWS = SLOTS * 16
MESH = pl.DeviceIdType.MESH


def slot_of(k):
    if k == 32:
        return 16
    if k % 4 == 0:
        return k // 4
    if k % 4 == 2:
        return 8 + k // 4
    return 17 + k // 4


HELD = [k for k in range(64) if k % 4 == 1 or (k % 2 == 0 and k <= 32)]


def tables():
    r = np.arange(TOK)
    angle = 2.0 * math.pi * ((r[:, None] * r[None, :]) % TOK) / TOK
    c, s = np.cos(angle), np.sin(angle)
    forward = np.block([[c, -s], [s, c]])
    inverse = np.block([[c, s], [-s, c]])

    def halves(m):
        hi = m.astype(np.float32).astype(jnp.bfloat16)
        lo = (m - hi.astype(np.float64)).astype(np.float32).astype(jnp.bfloat16)
        return np.stack([hi, lo])

    twist = np.zeros((2, 40, TOK), np.float32)
    for k in HELD:
        a = 2.0 * math.pi * k * r / SEQ
        twist[0, slot_of(k)] = np.cos(a)
        twist[1, slot_of(k)] = np.sin(a)
    return halves(forward), halves(inverse), twist


def p_add(a, b):
    if a is None:
        return b
    return a if b is None else a + b


def p_sub(a, b):
    if b is None:
        return a
    return -b if a is None else a - b


def c_add(a, b):
    return (p_add(a[0], b[0]), p_add(a[1], b[1]))


def c_sub(a, b):
    return (p_sub(a[0], b[0]), p_sub(a[1], b[1]))


def by_i(a):
    return (p_sub(None, a[1]), a[0])


def p_mul(a, f):
    return None if a is None or f == 0.0 else a * f


def turn(z, k, n):
    k = k % n
    if k == 0:
        return z
    if 4 * k == n:
        return by_i(z)
    if 2 * k == n:
        return c_sub((None, None), z)
    if 4 * k == 3 * n:
        return (z[1], p_sub(None, z[0]))
    c, s = math.cos(2 * math.pi * k / n), math.sin(2 * math.pi * k / n)
    return (
        p_sub(p_mul(z[0], c), p_mul(z[1], s)),
        p_add(p_mul(z[0], s), p_mul(z[1], c)),
    )


def four(z, sign):
    t0, t1 = c_add(z[0], z[2]), c_sub(z[0], z[2])
    t2, t3 = c_add(z[1], z[3]), by_i(c_sub(z[1], z[3]))
    if sign < 0:
        return [c_add(t0, t2), c_sub(t1, t3), c_sub(t0, t2), c_add(t1, t3)]
    return [c_add(t0, t2), c_add(t1, t3), c_sub(t0, t2), c_sub(t1, t3)]


def blocks_forward(get, put):
    t = {}
    for h in range(2):
        for c in range(2):
            for x in range(4):
                v = [get(h, c, y, x) for y in range(4)]
                s02, d02 = v[0] + v[2], v[0] - v[2]
                s13, d13 = v[1] + v[3], v[1] - v[3]
                a = 8 * h + 2 * x + c
                t[0, h, c, x] = (s02 + s13, None)
                t[1, h, c, x] = turn((d02, -d13), -a, 64)
                t[2, h, c, x] = turn((s02 - s13, None), -2 * a, 64)
    for ky in range(3):
        for kh in range(2):
            halves = []
            for c in range(2):
                z = []
                for x in range(4):
                    if kh == 0:
                        z.append(c_add(t[ky, 0, c, x], t[ky, 1, c, x]))
                    else:
                        z.append(turn(c_sub(t[ky, 0, c, x], t[ky, 1, c, x]), -(2 * x + c), 16))
                z = four(z, -1)
                if c == 1:
                    z = [turn(z[kx], -kx, 8) for kx in range(4)]
                halves.append(z)
            for kx in range(4):
                k = ky + 4 * kh + 8 * kx
                put(slot_of(k), c_add(halves[0][kx], halves[1][kx]))
                if ky == 1 or k == 0:
                    put(slot_of(k + 32), c_sub(halves[0][kx], halves[1][kx]))


def blocks_inverse(get, put):
    u = {}
    for ky in range(3):
        for kh in range(2):
            lanes = [[], []]
            for kx in range(4):
                k = ky + 4 * kh + 8 * kx
                z = get(slot_of(k))
                if ky == 1 or k == 0:
                    w = get(slot_of(k + 32))
                    first, second = c_add(z, w), c_sub(z, w)
                else:
                    first, second = z, z
                lanes[0].append(first)
                lanes[1].append(turn(second, kx, 8))
            for c in range(2):
                z = four(lanes[c], 1)
                for x in range(4):
                    u[ky, kh, c, x] = turn(z[x], (2 * x + c) * kh, 16)
    for c in range(2):
        for x in range(4):
            for h in range(2):
                a = 8 * h + 2 * x + c
                join = c_add if h == 0 else c_sub
                u0 = join(u[0, 0, c, x], u[0, 1, c, x])[0]
                u1 = turn(join(u[1, 0, c, x], u[1, 1, c, x]), a, 64)
                u2 = turn(join(u[2, 0, c, x], u[2, 1, c, x]), 2 * a, 64)[0]
                even, odd = u0 + u2, u0 - u2
                put(h, c, 0, x, even + u1[0])
                put(h, c, 1, x, odd - u1[1])
                put(h, c, 2, x, even - u1[0])
                put(h, c, 3, x, odd + u1[1])


def split(v):
    hi = v.astype(BF16)
    return hi, (v - hi.astype(F32)).astype(BF16)


def dot(a, b):
    return jnp.dot(a, b, preferred_element_type=F32)


def dot_t(a, b):
    return lax.dot_general(a, b, (((1,), (1,)), ((), ())), preferred_element_type=F32)


def dot3(hi, lo, m):
    return dot(hi, m[0]) + dot(lo, m[0]) + dot(hi, m[1])


def kernel(
    h_values, h_queries, h_out_grad, h_weight, h_filt, h_fwd, h_inv, h_twist,
    o_query, o_value, o_gf, o_rd,
    values, queries, out_grad, w_in, filt, m_fwd, m_inv, twist,
    g_gated, qt, val_t, gm_t, fil_t,
    r1v, r1g, f1, xv, xg, hx, hrev, hs, lhi, llo, spec_v, spec_g, back,
    ymix, ygv, r2m, r2v, mix_t, gv_t, gp, gpx, gs, gr, gfi,
    k_query, k_value, s_out, s_gfo, qx, mx, og_all, gat_all, wb, ry, sc, rc, sd, rd,
    s_in, s_ogs, s_ogr, s_qxs, s_qxr, s_mxs, s_mxr, s_gxr, s_gxs, s_gps, s_gpr,
    s1vs, s1vr, s1gs, s1gr, s1fs, s1fr,
    s2vs, s2vr, s2gs, s2gr, s2fs, s2fr, s3fs, s3fr,
    sams, samr, savs, savr, sbms, sbmr, sbvs, sbvr,
    sags, sagr, sbgs, sbgr,
    srys, sryr, srcs, srcr, srds, srdr,
):
    n = lax.axis_index("dp")
    ctx = lax.axis_index("ctx")
    y, h = lax.div(ctx, 16), lax.rem(lax.div(ctx, 8), 2)
    x, c = lax.rem(lax.div(ctx, 2), 4), lax.rem(ctx, 2)
    p, z = y * 4 + x, h * 4 + n
    hc = h * 2 + c
    active = n != 2
    unit = z - (z >= 3).astype(jnp.int32) - (z >= 7).astype(jnp.int32)

    def at(pp, zz, cc):
        return (
            lax.rem(zz, 4),
            lax.div(pp, 4) * 16 + lax.div(zz, 4) * 8 + lax.rem(pp, 4) * 2 + cc,
        )

    def remote(src, dst, ss, rs, dev):
        return pltpu.make_async_remote_copy(
            src_ref=src, dst_ref=dst, send_sem=ss, recv_sem=rs,
            device_id=dev, device_id_type=MESH,
        )

    def local(src, dst, sem):
        pltpu.make_async_copy(src, dst, sem).start()

    def landed(dst, sem):
        pltpu.make_async_copy(dst, dst, sem).wait()

    def left(src, sem):
        pltpu.make_async_copy(src, src, sem).wait()

    def rounds(lo, hi, body):
        lax.fori_loop(lo, hi, lambda i, carry: (body(i), carry)[1], 0)

    def place(i):
        return lax.rem(y + lax.div(i, 4), 4) * 4 + lax.rem(x + lax.rem(i, 4), 4)

    def over_p(send):
        rounds(1, 16, lambda i: send(place(i)))

    inputs = [
        pltpu.make_async_copy(src, dst, s_in.at[i])
        for i, (src, dst) in enumerate(
            [
                (h_values, values), (h_queries, queries), (h_out_grad, out_grad),
                (h_weight, w_in), (h_filt, filt), (h_fwd, m_fwd), (h_inv, m_inv),
                (h_twist, twist),
            ]
        )
    ]
    for copy in inputs:
        copy.start()

    barrier = pltpu.get_barrier_semaphore()

    def greet(dev):
        pl.semaphore_signal(barrier, inc=1, device_id=dev, device_id_type=MESH)

    over_p(lambda q: greet(at(q, z, c)))
    rounds(
        1, 16,
        lambda i: greet(
            at(p, lax.rem(z + lax.div(i, 2), 8), lax.rem(c + lax.rem(i, 2), 2))
        ),
    )
    rounds(1, 4, lambda i: greet(at(y * 4 + lax.rem(x + i, 4), z, 1 - c)))

    def turn_in(src, dst):
        for j in range(D // 128):
            dst[j * 128 : (j + 1) * 128, :] = src[:, j * 128 : (j + 1) * 128].T

    inputs[0].wait()
    turn_in(values, val_t)
    pl.semaphore_wait(barrier, 33)

    def hop1(src, dst, ss, rs):
        local(src.at[pl.ds(p * 96, 96)], dst.at[p], rs.at[p])
        over_p(
            lambda q: remote(
                src.at[pl.ds(q * 96, 96)], dst.at[p], ss.at[q], rs.at[p], at(q, z, c)
            ).start()
        )

    def hop1_done(src, ss):
        over_p(lambda q: left(src.at[pl.ds(q * 96, 96)], ss.at[q]))

    hop1(val_t, r1v, s1vs, s1vr)

    inputs[1].wait()
    for j in range(D // 128):
        piece = queries[:, j * 128 : (j + 1) * 128].T
        for g in range(8):
            k = j * 8 + g
            qt[k // 12, (k // 3) % 4, (k % 3) * 16 : (k % 3) * 16 + 16, :] = (
                piece[g * 16 : g * 16 + 16]
            )
    inputs[2].wait()
    inputs[3].wait()

    def gated_rows(i):
        rows = pl.ds(pl.multiple_of(i * 256, 256), 256)
        g = dot_t(w_in[rows, :], out_grad[...])
        g_gated[rows, :] = g

    rounds(0, 6, gated_rows)
    gm_t[...] = (g_gated[...] * qt[...].reshape(D, TOK).astype(F32)).astype(BF16)

    inputs[4].wait()
    for part in range(2):
        turn_in(filt.at[part], fil_t.at[part])
    two = jnp.logical_or(n == 0, n == 3)
    sz = [
        lax.rem(z + 3 * (n == 2).astype(jnp.int32), 8),
        lax.rem(z + 8 + (n == 3).astype(jnp.int32) - (n == 0).astype(jnp.int32), 8),
    ]

    def unit_at(zz):
        return zz - (zz >= 3).astype(jnp.int32) - (zz >= 7).astype(jnp.int32)

    def f_src(k, q):
        return fil_t.at[:, pl.ds(q * 96 + unit_at(sz[k]) * 16, 16), :]

    def filter_hop1(k):
        local(f_src(k, p), f1.at[k, p], s1fr.at[k, p])
        over_p(
            lambda q: remote(
                f_src(k, q), f1.at[k, p], s1fs.at[k, q], s1fr.at[k, p], at(q, z, c)
            ).start()
        )

    filter_hop1(0)
    pl.when(two)(lambda: filter_hop1(1))
    hop1(gm_t, r1g, s1gs, s1gr)

    core = lax.div(n, 2)

    def z_of(u):
        return u + (u >= 2).astype(jnp.int32) + (u >= 5).astype(jnp.int32)

    def hop2(r1, r1_sem, dst, ss, rs):
        def row(j):
            yy = lax.rem(y + j, 4)
            blocks = pl.ds(yy * 4, 4)
            rounds(0, 4, lambda q: landed(r1.at[yy * 4 + q], r1_sem.at[yy * 4 + q]))
            slot = dst.at[lax.rem(n, 2), hc, blocks]
            sem = rs.at[lax.rem(n, 2), hc]

            def send(i):
                u = lax.rem(unit + i, 6)
                zz = z_of(u)
                src = r1.at[blocks, pl.ds(u * 16, 16), :]
                mine = jnp.logical_and(zz == z, core == c)

                @pl.when(mine)
                def _():
                    local(src, slot, sem)

                @pl.when(jnp.logical_not(mine))
                def _():
                    remote(src, slot, ss.at[u], sem, at(p, zz, core)).start()

            rounds(0, 6, send)

        rounds(0, 4, row)

    def hop2_done(r1, ss):
        def done(u):
            mine = jnp.logical_and(z_of(u) == z, core == c)

            @pl.when(jnp.logical_not(mine))
            def _():
                left(r1.at[:, pl.ds(u * 16, 16), :], ss.at[u])

        rounds(0, 6, done)

    hop2(r1v, s1vr, xv, s2vs, s2vr)

    def filter_hop2(k):
        rounds(0, 16, lambda q: landed(f1.at[k, q], s1fr.at[k, q]))
        mine = sz[k] == z

        @pl.when(mine)
        def _():
            local(f1.at[k], hx.at[h, c], s2fr.at[h])

        @pl.when(jnp.logical_not(mine))
        def _():
            remote(f1.at[k], hx.at[h, c], s2fs.at[k], s2fr.at[h], at(p, sz[k], c)).start()

    def filter_hop2_done(k):
        @pl.when(sz[k] != z)
        def _():
            left(f1.at[k], s2fs.at[k])

    filter_hop2(0)
    pl.when(two)(lambda: filter_hop2(1))
    hop2(r1g, s1gr, xg, s2gs, s2gr)

    other = at(p, z, 1 - c)

    def og_send(i):
        xx, cc = lax.rem(x + lax.div(i, 2), 4), lax.rem(c + lax.rem(i, 2), 2)
        half = pl.ds(pl.multiple_of(cc * 768, 768), 768)
        slot = og_all.at[x, pl.ds(pl.multiple_of(c * 128, 128), 128)]
        remote(
            out_grad.at[:, half], slot, s_ogs.at[i], s_ogr.at[x, c], at(y * 4 + xx, z, cc)
        ).start()

    def qx_send(i):
        xx = lax.rem(x + i, 4)
        remote(
            qt.at[:, xx], qx.at[x], s_qxs.at[i], s_qxr.at[x], at(y * 4 + xx, z, c)
        ).start()

    rounds(1, 4, qx_send)
    local(qt.at[:, x], qx.at[x], s_qxr.at[x])

    own_half = pl.ds(pl.multiple_of(c * 768, 768), 768)
    own_depth = pl.ds(pl.multiple_of(c * 128, 128), 128)
    local(out_grad.at[:, own_half], og_all.at[x, own_depth], s_ogr.at[x, c])
    rounds(1, 8, og_send)

    def transform(src, spec, nn):
        def get(hh, cc, yy, xx):
            return src[nn, 2 * hh + cc, 4 * yy + xx].astype(F32)

        def put(s, v):
            co, si = twist[0, s : s + 1, :], twist[1, s : s + 1, :]
            re, im = v
            if im is None:
                out = (re * co, -(re * si))
            else:
                out = (re * co + im * si, im * co - re * si)
            for j in range(2):
                hi, lo = split(out[j])
                lhi[s * 16 : s * 16 + 16, j * 128 : j * 128 + 128] = hi
                llo[s * 16 : s * 16 + 16, j * 128 : j * 128 + 128] = lo

        blocks_forward(get, put)
        spec[nn] = dot3(lhi[...], llo[...], m_fwd)

    def untransform(product, dst, nn):
        for j, v in enumerate(product):
            hi, lo = split(v)
            lhi[:, j * 128 : j * 128 + 128] = hi
            llo[:, j * 128 : j * 128 + 128] = lo
        back[...] = dot3(lhi[...], llo[...], m_inv)

        def get(s):
            co = twist[0, s : s + 1, :] * (1.0 / SEQ)
            si = twist[1, s : s + 1, :] * (1.0 / SEQ)
            re = back[s * 16 : s * 16 + 16, :128]
            im = back[s * 16 : s * 16 + 16, 128:]
            return (re * co - im * si, im * co + re * si)

        def put(hh, cc, yy, xx, v):
            dst[nn, 2 * hh + cc, 4 * yy + xx] = v.astype(BF16)

        blocks_inverse(get, put)

    def hop_a(src, dst, ss, rs, nn):
        def send(j):
            i = nn * 4 + j
            hh, cc = lax.rem(lax.div(i, 2), 2), lax.rem(i, 2)
            zz = hh * 4 + 2 * c + nn
            mine = jnp.logical_and(zz == z, cc == c)

            @pl.when(mine)
            def _():
                local(src.at[nn, 2 * hh + cc], dst.at[unit], rs.at[unit])

            @pl.when(jnp.logical_not(mine))
            def _():
                remote(
                    src.at[nn, 2 * hh + cc], dst.at[unit], ss.at[i], rs.at[unit], at(p, zz, cc)
                ).start()

        rounds(0, 4, send)

    def hop_a_done(src, ss):
        def done(i):
            nn, hh, cc = lax.div(i, 4), lax.rem(lax.div(i, 2), 2), lax.rem(i, 2)
            zz = hh * 4 + 2 * c + nn
            mine = jnp.logical_and(zz == z, cc == c)

            @pl.when(jnp.logical_not(mine))
            def _():
                left(src.at[nn, 2 * hh + cc], ss.at[i])

        rounds(0, 8, done)

    def hop_b(r2, r2_sem, dst, ss, rs):
        def relay(i):
            u = lax.rem(unit + i, 6)
            if r2_sem is not None:
                landed(r2.at[u], r2_sem.at[u])
            local(r2.at[u, p], dst.at[p, u], rs.at[p])
            over_p(
                lambda q: remote(
                    r2.at[u, q], dst.at[p, u], ss.at[q], rs.at[p], at(q, z, c)
                ).start()
            )

        rounds(0, 6, relay)

    def hop_b_done(r2, ss):
        over_p(lambda q: left(r2.at[:, q], ss.at[q]))

    ident = (
        lax.broadcasted_iota(jnp.int32, (128, 128), 0)
        == lax.broadcasted_iota(jnp.int32, (128, 128), 1)
    ).astype(F32).astype(BF16)
    flip = (
        lax.broadcasted_iota(jnp.int32, (128, 128), 0)
        == 127 - lax.broadcasted_iota(jnp.int32, (128, 128), 1)
    ).astype(F32).astype(BF16)

    for copy in inputs[5:]:
        copy.wait()

    @pl.when(active)
    def _():
        for hh in range(2):
            landed(hx.at[hh, c], s2fr.at[hh])
            remote(hx.at[hh, c], hx.at[hh, c], s3fs.at[hh], s3fr.at[hh], other).start()
        for hh in range(2):
            landed(hx.at[hh, 1 - c], s3fr.at[hh])

        def raw(k):
            return hx[(k >> 3) & 1, k & 1, (k >> 4) * 4 + ((k >> 1) & 3)]

        for k in HELD:
            s = slot_of(k)
            if k % 32:
                hrev[s * 32 : s * 32 + 32, :] = raw(64 - k).reshape(32, 128)
            else:
                hrev[s * 32 : s * 32 + 32, :] = jnp.zeros((32, 128), BF16)
        turned = dot(hrev[...], flip).reshape(SLOTS, 32, 128)
        for k in HELD:
            s = slot_of(k)
            v = raw(k).astype(F32)
            hs[s * 16 : s * 16 + 16, :128] = v[0] + turned[s, :16]
            hs[s * 16 : s * 16 + 16, 128:] = v[1] - turned[s, 16:]

        def values_part(nn):
            rounds(0, 4, lambda i: landed(xv.at[nn, i], s2vr.at[nn, i]))
            transform(xv, spec_v, nn)
            hr, hi = hs[:, :128], hs[:, 128:]
            vr, vi = spec_v[nn, :, :128], spec_v[nn, :, 128:]
            untransform((hr * vr - hi * vi, hr * vi + hi * vr), ymix, nn)
            hop_a(ymix, r2m, sams, samr, nn)

        rounds(0, 2, values_part)

        def grads_part(nn):
            rounds(0, 4, lambda i: landed(xg.at[nn, i], s2gr.at[nn, i]))
            transform(xg, spec_g, nn)
            hr, hi = hs[:, :128], hs[:, 128:]
            gr_, gi = spec_g[nn, :, :128], spec_g[nn, :, 128:]
            untransform((gr_ * hr + gi * hi, gi * hr - gr_ * hi), ygv, nn)
            hop_a(ygv, r2v, savs, savr, nn)

        rounds(0, 2, grads_part)
        re, im = 0.0, 0.0
        for nn in range(2):
            vr, vi = spec_v[nn, :, :128], spec_v[nn, :, 128:]
            gr_, gi = spec_g[nn, :, :128], spec_g[nn, :, 128:]
            re = re + (gr_ * vr + gi * vi)
            im = im + (gi * vr - gr_ * vi)
        gp[:, :128] = re * (1.0 / SEQ)
        gp[:, 128:] = im * (1.0 / SEQ)
        gp_rows = pl.ds(pl.multiple_of((1 - c) * 256, 256), 272)
        remote(gp.at[gp_rows], gpx, s_gps, s_gpr, other).start()

    def mixed_share(i):
        u = lax.rem(unit + i, 6)
        landed(r2m.at[u], samr.at[u])
        xx = 2 * lax.rem(x, 2) + lax.div(u, 3)
        yh = y * 2 + lax.div(x, 2)
        slot = mx.at[:, yh, pl.ds(pl.multiple_of(lax.rem(u, 3) * 16, 16), 16), :]

        def send(j):
            yy = lax.rem(y + j, 4)
            src = r2m.at[u, pl.ds(yy * 4, 4)]
            mine = jnp.logical_and(j == 0, xx == x)

            @pl.when(mine)
            def _():
                local(src, slot, s_mxr.at[yh])

            @pl.when(jnp.logical_not(mine))
            def _():
                remote(
                    src, slot, s_mxs.at[u, yy], s_mxr.at[yh], at(yy * 4 + xx, z, c)
                ).start()

        rounds(0, 4, send)

    def mixed_share_done(u):
        xx = 2 * lax.rem(x, 2) + lax.div(u, 3)

        def done(yy):
            mine = jnp.logical_and(yy == y, xx == x)

            @pl.when(jnp.logical_not(mine))
            def _():
                left(r2m.at[u, pl.ds(yy * 4, 4)], s_mxs.at[u, yy])

        rounds(0, 4, done)

    hop1_done(val_t, s1vs)
    hop1_done(gm_t, s1gs)
    over_p(lambda q: left(f_src(0, q), s1fs.at[0, q]))
    filter_hop2_done(0)

    @pl.when(two)
    def _():
        over_p(lambda q: left(f_src(1, q), s1fs.at[1, q]))
        filter_hop2_done(1)

    hop2_done(r1v, s2vs)
    hop2_done(r1g, s2gs)
    rounds(1, 8, lambda i: left(og_all.at[x, own_depth], s_ogs.at[i]))
    rounds(1, 4, lambda i: left(qx.at[0], s_qxs.at[i]))

    rounds(0, 6, mixed_share)

    @pl.when(active)
    def _():
        landed(gpx, s_gpr)

        def fill(i):
            q, hh = lax.div(i, 2), lax.rem(i, 2)
            a = lax.div(q, 4) * 16 + hh * 8 + lax.rem(q, 4) * 2 + c
            low = lax.rem(a, 4)
            straight = jnp.logical_or(low == 1, jnp.logical_and(c == 0, a <= 32))
            k = jnp.where(straight, a, 64 - a)
            base = jnp.where(lax.rem(k, 4) == 1, 17, jnp.where(lax.rem(k, 4) == 2, 8, 0))
            s = jnp.where(k == 32, 16, base + lax.div(k, 4))
            total = gp[pl.ds(pl.multiple_of(s * 16, 16), 16), :] + gpx[
                pl.ds(pl.multiple_of(s * 16 - 256 * c, 16), 16), :
            ]
            gs[q, hh, 0] = total[:, :128].astype(BF16)
            gs[q, hh, 1] = total[:, 128:].astype(BF16)

        rounds(0, 32, fill)
        local(gs.at[p], gr.at[p], sagr.at[p])
        over_p(
            lambda q: remote(gs.at[q], gr.at[p], sags.at[q], sagr.at[p], at(q, z, c)).start()
        )

    rounds(0, 8, lambda i: landed(mx.at[:, i], s_mxr.at[i]))

    def gate(i):
        xx = lax.rem(x + i, 4)
        landed(qx.at[xx], s_qxr.at[xx])
        gat_all[xx, :, :, own_depth] = (qx[xx].astype(F32) * mx[xx].astype(F32)).astype(BF16)
        here = gat_all.at[xx, :, :, own_depth]
        remote(here, here, s_gxs.at[xx], s_gxr.at[xx], other).start()

    rounds(0, 4, gate)

    @pl.when(active)
    def _():
        rounds(0, 16, lambda q: landed(gr.at[q], sagr.at[q]))
        local(gr.at[:, h], gfi.at[:, unit], sbgr.at[unit])
        first = [
            h * 4 + jnp.where(n == 0, 1, jnp.where(n == 1, 0, 2)),
            h * 4 + jnp.where(n == 3, 1, 2),
            (1 - h) * 4 + jnp.where(n == 0, 1, 0),
            (1 - h) * 4 + jnp.where(n == 3, 2, 3),
        ]
        for k, zz in enumerate(first):
            half = h if k < 2 else 1 - h
            remote(
                gr.at[:, half], gfi.at[:, unit], sbgs.at[k], sbgr.at[unit], at(p, zz, c)
            ).start()

    mate = h * 4 + n + 1 - 2 * lax.rem(n, 2)
    passes = [
        (h * 4 + 1, n == 2), (h * 4, n == 2), (h * 4 + 3, n == 1),
        ((1 - h) * 4 + 3, jnp.logical_or(n == 0, n == 2)),
        ((1 - h) * 4, jnp.logical_or(n == 1, n == 3)),
        ((1 - h) * 4 + 1, jnp.logical_or(n == 0, n == 3)),
    ]

    def gf_pass(k):
        source, here = passes[k]
        u = unit_at(source)

        @pl.when(here)
        def _():
            landed(gfi.at[:, u], sbgr.at[u])
            remote(
                gfi.at[:, u], gfi.at[:, u], sbgs.at[4 + k], sbgr.at[u], at(p, mate, c)
            ).start()

    def gf_last(k):
        source, here = passes[k]
        u = unit_at(source)

        @pl.when(jnp.logical_not(here))
        def _():
            landed(gfi.at[:, u], sbgr.at[u])

        pltpu.make_async_copy(gfi.at[:, u], o_gf.at[:, u], s_gfo.at[k]).start()

    def gf_left(k):
        source, here = passes[k]
        u = unit_at(source)

        @pl.when(here)
        def _():
            left(gfi.at[:, u], sbgs.at[4 + k])


    other_depth = pl.ds(pl.multiple_of((1 - c) * 128, 128), 128)

    def w_wait(xx):
        landed(gat_all.at[xx, :, :, other_depth], s_gxr.at[xx])
        landed(og_all.at[xx, own_depth], s_ogr.at[xx, c])
        landed(og_all.at[xx, other_depth], s_ogr.at[xx, 1 - c])

    rounds(0, 4, w_wait)

    def weight_rows(i):
        yy = lax.rem(y + i, 4)
        total = dot(gat_all[0, pl.ds(yy * 2, 2)].reshape(96, 256), og_all[0])
        for xx in range(1, 4):
            total = total + dot(gat_all[xx, pl.ds(yy * 2, 2)].reshape(96, 256), og_all[xx])
        wb[yy] = total.astype(BF16).reshape(2, 48, 768)

        @pl.when(i < 4)
        def _():
            remote(wb.at[yy], ry.at[y], srys.at[i], sryr.at[y], at(yy * 4 + x, z, c)).start()

    rounds(1, 5, weight_rows)
    hop_b(r2m, None, mix_t, sbms, sbmr)
    hop_b(r2v, savr, gv_t, sbvs, sbvr)
    rounds(1, 4, lambda i: landed(ry.at[lax.rem(y + i, 4)], sryr.at[lax.rem(y + i, 4)]))
    total = wb[y].astype(F32)
    for i in range(1, 4):
        total = total + ry[lax.rem(y + i, 4)].astype(F32)
    sc[...] = total.astype(BF16).reshape(2, 3, 16, 768)

    def rc_send(i):
        hh, t = lax.div(i, 3), lax.rem(i, 3)
        zz = hh * 4 + t

        @pl.when(zz == z)
        def _():
            local(sc.at[hh, t], rc.at[z], srcr.at[z])

        @pl.when(zz != z)
        def _():
            remote(sc.at[hh, t], rc.at[z], srcs.at[i], srcr.at[z], at(p, zz, c)).start()

    rounds(0, 6, rc_send)
    for k in range(6):
        gf_pass(k)
    rounds(0, 16, lambda q: landed(mix_t.at[q], sbmr.at[q]))
    gq = (g_gated[...] * mix_t[...].reshape(D, TOK).astype(F32)).astype(BF16)
    k_query[...] = dot_t(ident, gq).astype(BF16)
    query_out = pltpu.make_async_copy(k_query, o_query, s_out.at[0])
    query_out.start()

    rounds(0, 6, mixed_share_done)
    hop_b_done(r2m, sbms)
    rounds(0, 4, lambda i: left(gat_all.at[i, :, :, own_depth], s_gxs.at[i]))

    @pl.when(active)
    def _():
        for hh in range(2):
            left(hx.at[hh, c], s3fs.at[hh])
        hop_a_done(ymix, sams)
        hop_a_done(ygv, savs)
        left(gpx, s_gps)
        over_p(lambda q: left(gs.at[q], sags.at[q]))

    rounds(1, 4, lambda i: left(wb.at[0], srys.at[i]))
    rounds(0, 16, lambda q: landed(gv_t.at[q], sbvr.at[q]))
    k_value[...] = dot_t(ident, gv_t[...].reshape(D, TOK)).astype(BF16)
    value_out = pltpu.make_async_copy(k_value, o_value, s_out.at[1])
    value_out.start()
    owner = n < 3

    @pl.when(owner)
    def _():
        rounds(0, 8, lambda i: landed(rc.at[i], srcr.at[i]))
        total = rc[0].astype(F32)
        for i in range(1, 8):
            total = total + rc[i].astype(F32)
        sd[...] = total.astype(BF16)

        def send(i):
            nn, cc = lax.div(i, 2), lax.rem(i, 2)
            mine = jnp.logical_and(nn == n, cc == c)

            @pl.when(mine)
            def _():
                local(sd, rd.at[n, c], srdr.at[n, c])

            @pl.when(jnp.logical_not(mine))
            def _():
                remote(sd, rd.at[n, c], srds.at[i], srdr.at[n, c],
                       at(p, h * 4 + nn, cc)).start()

        rounds(0, 8, send)

    hop_b_done(r2v, sbvs)
    def rc_done(i):
        @pl.when(lax.div(i, 3) * 4 + lax.rem(i, 3) != z)
        def _():
            left(sd, srcs.at[i])

    rounds(0, 6, rc_done)

    for k in range(6):
        gf_last(k)
    for t in range(3):
        for cc in range(2):
            landed(rd.at[t, cc], srdr.at[t, cc])
    weight_out = pltpu.make_async_copy(rd, o_rd, s_out.at[3])
    weight_out.start()

    for copy in (query_out, value_out, weight_out):
        copy.wait()
    for k in range(6):
        left(gfi.at[:, 0], s_gfo.at[k])

    @pl.when(active)
    def _():
        rounds(0, 4, lambda k: left(gr.at[:, 0], sbgs.at[k]))

    for k in range(6):
        gf_left(k)

    @pl.when(owner)
    def _():
        def done(i):
            mine = jnp.logical_and(lax.div(i, 2) == n, lax.rem(i, 2) == c)

            @pl.when(jnp.logical_not(mine))
            def _():
                left(sd, srds.at[i])

        rounds(0, 8, done)


def finish(
    h_query, h_value, h_gf, h_rd, o_query, o_value, o_filter, o_weight,
    gfi, rd, k_query, k_value, k_filter, sem
):
    ctx = lax.axis_index("ctx")
    c = lax.rem(ctx, 2)
    gf_in = pltpu.make_async_copy(h_gf, gfi, sem.at[0])
    rd_in = pltpu.make_async_copy(h_rd, rd, sem.at[1])
    query_in = pltpu.make_async_copy(h_query, k_query, sem.at[2])
    value_in = pltpu.make_async_copy(h_value, k_value, sem.at[3])
    for copy in (gf_in, query_in, value_in, rd_in):
        copy.start()
    row = lax.broadcasted_iota(jnp.int32, (128, 128), 0)
    col = lax.broadcasted_iota(jnp.int32, (128, 128), 1)
    straight = jnp.logical_or(lax.rem(ctx, 4) == 1, jnp.logical_and(c == 0, ctx <= 32))
    pick = (row == jnp.where(straight, col, 127 - col)).astype(F32).astype(BF16)
    sign = jnp.where(straight, 1.0, -1.0)
    outs = [
        pltpu.make_async_copy(k_query, o_query, sem.at[6]),
        pltpu.make_async_copy(k_value, o_value, sem.at[7]),
    ]
    gf_in.wait()
    for copy, out in zip((query_in, value_in), outs):
        copy.wait()
        out.start()
    for part in range(2):
        value_part = dot_t(pick, gfi[:, :, part].reshape(D, TOK))
        k_filter[part] = value_part if part == 0 else value_part * sign
        out = pltpu.make_async_copy(k_filter.at[part], o_filter.at[part], sem.at[4 + part])
        out.start()
        outs.append(out)
    rd_in.wait()
    scale = 1.0 / math.sqrt(4 * SEQ)
    for cc in range(2):
        cols = slice(cc * 768, (cc + 1) * 768)

        @pl.when(c == 0)
        def _():
            o_weight[0:16, cols] = rd[0, cc].astype(F32) * scale
            o_weight[16:24, cols] = rd[1, cc].astype(F32)[0:8] * scale

        @pl.when(c == 1)
        def _():
            o_weight[0:8, cols] = rd[1, cc].astype(F32)[8:16] * scale
            o_weight[8:24, cols] = rd[2, cc].astype(F32) * scale

    for copy in outs:
        copy.wait()


def on_device(queries, values, out_grad, out_weight, filter_spec):
    m_fwd, m_inv, twist = tables()
    vmem = pl.BlockSpec(memory_space=pltpu.VMEM)
    dma = pltpu.SemaphoreType.DMA

    def held(*shape, dtype=BF16):
        return pltpu.VMEM(shape, dtype)

    scratch = [
        held(TOK, D), held(TOK, D), held(TOK, D), held(D, D), held(2, TOK, D),
        held(2, 256, 256), held(2, 256, 256), held(2, 40, TOK, dtype=F32),
        held(D, TOK, dtype=F32), held(8, 4, 48, TOK), held(D, TOK), held(D, TOK), held(2, D, TOK),
        held(16, 96, TOK), held(16, 96, TOK), held(2, 16, 2, 16, TOK),
        held(2, 4, 16, 16, TOK), held(2, 4, 16, 16, TOK), held(2, 2, 16, 2, 16, TOK),
        held(SLOTS * 32, TOK), held(ROWS, 256, dtype=F32),
        held(ROWS, 256), held(ROWS, 256),
        held(2, ROWS, 256, dtype=F32), held(2, ROWS, 256, dtype=F32), held(ROWS, 256, dtype=F32),
        held(2, 4, 16, 16, TOK), held(2, 4, 16, 16, TOK),
        held(6, 16, 16, TOK), held(6, 16, 16, TOK),
        held(16, 6, 16, TOK), held(16, 6, 16, TOK),
        held(ROWS, 256, dtype=F32), held(272, 256, dtype=F32),
        held(16, 2, 2, 16, TOK), held(16, 2, 2, 16, TOK), held(16, 6, 2, 16, TOK),
        held(TOK, D), held(TOK, D), dma((4,)), dma((6,)),
        held(4, 8, 48, TOK), held(4, 8, 48, TOK), held(4, 256, 768), held(4, 8, 48, 256),
        held(4, 2, 48, 768), held(4, 2, 48, 768),
        held(2, 3, 16, 768), held(8, 16, 768), held(16, 768), held(3, 2, 16, 768),
        dma((8,)), dma((8,)), dma((4, 2)), dma((4,)), dma((4,)), dma((6, 4)), dma((8,)), dma((4,)),
        dma((4,)), dma, dma,
        dma((16,)), dma((16,)), dma((16,)), dma((16,)), dma((2, 16)), dma((2, 16)),
        dma((6,)), dma((2, 4)), dma((6,)), dma((2, 4)), dma((2,)), dma((2,)), dma((2,)), dma((2,)),
        dma((8,)), dma((6,)), dma((8,)), dma((6,)), dma((16,)), dma((16,)), dma((16,)), dma((16,)),
        dma((16,)), dma((16,)), dma((10,)), dma((6,)),
        dma((4,)), dma((4,)), dma((6,)), dma((8,)), dma((8,)), dma((3, 2)),
    ]
    anywhere = pl.BlockSpec(memory_space=pl.ANY)
    parts = pl.pallas_call(
        kernel,
        out_shape=(
            jax.ShapeDtypeStruct((TOK, D), BF16),
            jax.ShapeDtypeStruct((TOK, D), BF16),
            jax.ShapeDtypeStruct((16, 6, 2, 16, TOK), BF16),
            jax.ShapeDtypeStruct((3, 2, 16, 768), BF16),
        ),
        in_specs=[pl.BlockSpec(memory_space=pl.ANY)] * 8,
        out_specs=(anywhere,) * 4,
        scratch_shapes=scratch,
        compiler_params=pltpu.CompilerParams(
            collective_id=0, has_side_effects=True, vmem_limit_bytes=60 * 2**20
        ),
    )(values[0], queries[0], out_grad[0], out_weight, filter_spec,
      jnp.asarray(m_fwd), jnp.asarray(m_inv), jnp.asarray(twist))
    grad_query, grad_value, grad_filter, grad_weight = pl.pallas_call(
        finish,
        out_shape=(
            jax.ShapeDtypeStruct((TOK, D), BF16),
            jax.ShapeDtypeStruct((TOK, D), BF16),
            jax.ShapeDtypeStruct((2, TOK, D), F32),
            jax.ShapeDtypeStruct((24, D), F32),
        ),
        in_specs=[anywhere] * 4,
        out_specs=(anywhere, anywhere, anywhere, vmem),
        scratch_shapes=[
            held(16, 6, 2, 16, TOK), held(3, 2, 16, 768), held(TOK, D), held(TOK, D),
            held(2, TOK, D, dtype=F32), dma((8,)),
        ],
        compiler_params=pltpu.CompilerParams(vmem_limit_bytes=60 * 2**20),
    )(*parts)
    return grad_query[None], grad_value[None], grad_filter, grad_weight


def solution(mesh):
    return jax.shard_map(
        on_device,
        mesh=mesh,
        in_specs=(
            P("dp", "ctx", None),
            P("dp", "ctx", None),
            P("dp", "ctx", None),
            P(),
            P(None, "ctx", None),
        ),
        out_specs=(
            P("dp", "ctx", None),
            P("dp", "ctx", None),
            P(None, "ctx", None),
            P("ctx", None),
        ),
        check_vma=False,
    )
```

```python
import functools
import math

import jax
import jax.numpy as jnp
import numpy as np
from jax import lax
from jax.experimental import pallas as pl
from jax.experimental.pallas import tpu as pltpu
from jax.sharding import PartitionSpec as P

F32 = jnp.float32
BF16 = jnp.bfloat16
TOK = 128
D = 1536
SEQ = 8192
SLOTS = 33
ROWS = SLOTS * 16
MESH = pl.DeviceIdType.MESH


def slot_of(k):
    if k == 32:
        return 16
    if k % 4 == 0:
        return k // 4
    if k % 4 == 2:
        return 8 + k // 4
    return 17 + k // 4


HELD = [k for k in range(64) if k % 4 == 1 or (k % 2 == 0 and k <= 32)]


def tables():
    r = np.arange(TOK)
    angle = 2.0 * math.pi * ((r[:, None] * r[None, :]) % TOK) / TOK
    c, s = np.cos(angle), np.sin(angle)
    forward = np.block([[c, -s], [s, c]])
    inverse = np.block([[c, s], [-s, c]])

    def halves(m):
        hi = m.astype(np.float32).astype(jnp.bfloat16)
        lo = (m - hi.astype(np.float64)).astype(np.float32).astype(jnp.bfloat16)
        return np.stack([hi, lo])

    twist = np.zeros((2, 40, TOK), np.float32)
    for k in HELD:
        a = 2.0 * math.pi * k * r / SEQ
        twist[0, slot_of(k)] = np.cos(a)
        twist[1, slot_of(k)] = np.sin(a)
    return halves(forward), halves(inverse), twist


def p_add(a, b):
    if a is None:
        return b
    return a if b is None else a + b


def p_sub(a, b):
    if b is None:
        return a
    return -b if a is None else a - b


def c_add(a, b):
    return (p_add(a[0], b[0]), p_add(a[1], b[1]))


def c_sub(a, b):
    return (p_sub(a[0], b[0]), p_sub(a[1], b[1]))


def by_i(a):
    return (p_sub(None, a[1]), a[0])


def p_mul(a, f):
    return None if a is None or f == 0.0 else a * f


def turn(z, k, n):
    k = k % n
    if k == 0:
        return z
    if 4 * k == n:
        return by_i(z)
    if 2 * k == n:
        return c_sub((None, None), z)
    if 4 * k == 3 * n:
        return (z[1], p_sub(None, z[0]))
    c, s = math.cos(2 * math.pi * k / n), math.sin(2 * math.pi * k / n)
    return (
        p_sub(p_mul(z[0], c), p_mul(z[1], s)),
        p_add(p_mul(z[0], s), p_mul(z[1], c)),
    )


def four(z, sign):
    t0, t1 = c_add(z[0], z[2]), c_sub(z[0], z[2])
    t2, t3 = c_add(z[1], z[3]), by_i(c_sub(z[1], z[3]))
    if sign < 0:
        return [c_add(t0, t2), c_sub(t1, t3), c_sub(t0, t2), c_add(t1, t3)]
    return [c_add(t0, t2), c_add(t1, t3), c_sub(t0, t2), c_sub(t1, t3)]


def blocks_forward(get, put):
    t = {}
    for h in range(2):
        for c in range(2):
            for x in range(4):
                v = [get(h, c, y, x) for y in range(4)]
                s02, d02 = v[0] + v[2], v[0] - v[2]
                s13, d13 = v[1] + v[3], v[1] - v[3]
                a = 8 * h + 2 * x + c
                t[0, h, c, x] = (s02 + s13, None)
                t[1, h, c, x] = turn((d02, -d13), -a, 64)
                t[2, h, c, x] = turn((s02 - s13, None), -2 * a, 64)
    for ky in range(3):
        for kh in range(2):
            halves = []
            for c in range(2):
                z = []
                for x in range(4):
                    if kh == 0:
                        z.append(c_add(t[ky, 0, c, x], t[ky, 1, c, x]))
                    else:
                        z.append(turn(c_sub(t[ky, 0, c, x], t[ky, 1, c, x]), -(2 * x + c), 16))
                z = four(z, -1)
                if c == 1:
                    z = [turn(z[kx], -kx, 8) for kx in range(4)]
                halves.append(z)
            for kx in range(4):
                k = ky + 4 * kh + 8 * kx
                put(slot_of(k), c_add(halves[0][kx], halves[1][kx]))
                if ky == 1 or k == 0:
                    put(slot_of(k + 32), c_sub(halves[0][kx], halves[1][kx]))


def blocks_inverse(get, put):
    u = {}
    for ky in range(3):
        for kh in range(2):
            lanes = [[], []]
            for kx in range(4):
                k = ky + 4 * kh + 8 * kx
                z = get(slot_of(k))
                if ky == 1 or k == 0:
                    w = get(slot_of(k + 32))
                    first, second = c_add(z, w), c_sub(z, w)
                else:
                    first, second = z, z
                lanes[0].append(first)
                lanes[1].append(turn(second, kx, 8))
            for c in range(2):
                z = four(lanes[c], 1)
                for x in range(4):
                    u[ky, kh, c, x] = turn(z[x], (2 * x + c) * kh, 16)
    for c in range(2):
        for x in range(4):
            for h in range(2):
                a = 8 * h + 2 * x + c
                join = c_add if h == 0 else c_sub
                u0 = join(u[0, 0, c, x], u[0, 1, c, x])[0]
                u1 = turn(join(u[1, 0, c, x], u[1, 1, c, x]), a, 64)
                u2 = turn(join(u[2, 0, c, x], u[2, 1, c, x]), 2 * a, 64)[0]
                even, odd = u0 + u2, u0 - u2
                put(h, c, 0, x, even + u1[0])
                put(h, c, 1, x, odd - u1[1])
                put(h, c, 2, x, even - u1[0])
                put(h, c, 3, x, odd + u1[1])


def split(v):
    hi = v.astype(BF16)
    return hi, (v - hi.astype(F32)).astype(BF16)


def dot(a, b):
    return jnp.dot(a, b, preferred_element_type=F32)


def dot_t(a, b):
    return lax.dot_general(a, b, (((1,), (1,)), ((), ())), preferred_element_type=F32)


def dot3(hi, lo, m):
    return dot(hi, m[0]) + dot(lo, m[0]) + dot(hi, m[1])


def kernel(
    h_values, h_queries, h_out_grad, h_weight, h_filt, h_fwd, h_inv, h_twist,
    o_query, o_value, o_gf, o_rd,
    values, queries, out_grad, w_in, filt, m_fwd, m_inv, twist,
    g_gated, qt, val_t, gm_t, fil_t,
    r1v, r1g, f1, xv, xg, hx, hrev, hs, lhi, llo, spec_v, spec_g, back,
    ymix, ygv, r2m, r2v, mix_t, gv_t, gp, gpx, gs, gr, gfi,
    k_query, k_value, s_out, s_gfo, qx, mx, og_all, gat_all, wb, ry, sc, rc, sd, rd,
    s_in, s_ogs, s_ogr, s_qxs, s_qxr, s_mxs, s_mxr, s_gxr, s_gxs, s_gps, s_gpr,
    s1vs, s1vr, s1gs, s1gr, s1fs, s1fr,
    s2vs, s2vr, s2gs, s2gr, s2fs, s2fr, s3fs, s3fr,
    sams, samr, savs, savr, sbms, sbmr, sbvs, sbvr,
    sags, sagr, sbgs, sbgr,
    srys, sryr, srcs, srcr, srds, srdr,
):
    n = lax.axis_index("dp")
    ctx = lax.axis_index("ctx")
    y, h = lax.div(ctx, 16), lax.rem(lax.div(ctx, 8), 2)
    x, c = lax.rem(lax.div(ctx, 2), 4), lax.rem(ctx, 2)
    p, z = y * 4 + x, h * 4 + n
    hc = h * 2 + c
    active = n != 2
    unit = z - (z >= 3).astype(jnp.int32) - (z >= 7).astype(jnp.int32)

    def at(pp, zz, cc):
        return (
            lax.rem(zz, 4),
            lax.div(pp, 4) * 16 + lax.div(zz, 4) * 8 + lax.rem(pp, 4) * 2 + cc,
        )

    def remote(src, dst, ss, rs, dev):
        return pltpu.make_async_remote_copy(
            src_ref=src, dst_ref=dst, send_sem=ss, recv_sem=rs,
            device_id=dev, device_id_type=MESH,
        )

    def local(src, dst, sem):
        pltpu.make_async_copy(src, dst, sem).start()

    def landed(dst, sem):
        pltpu.make_async_copy(dst, dst, sem).wait()

    def left(src, sem):
        pltpu.make_async_copy(src, src, sem).wait()

    def rounds(lo, hi, body):
        lax.fori_loop(lo, hi, lambda i, carry: (body(i), carry)[1], 0)

    def place(i):
        return lax.rem(y + lax.div(i, 4), 4) * 4 + lax.rem(x + lax.rem(i, 4), 4)

    def over_p(send):
        rounds(1, 16, lambda i: send(place(i)))

    inputs = [
        pltpu.make_async_copy(src, dst, s_in.at[i])
        for i, (src, dst) in enumerate(
            [
                (h_values, values), (h_queries, queries), (h_out_grad, out_grad),
                (h_weight, w_in), (h_filt, filt), (h_fwd, m_fwd), (h_inv, m_inv),
                (h_twist, twist),
            ]
        )
    ]
    for copy in inputs:
        copy.start()

    barrier = pltpu.get_barrier_semaphore()

    def greet(dev):
        pl.semaphore_signal(barrier, inc=1, device_id=dev, device_id_type=MESH)

    over_p(lambda q: greet(at(q, z, c)))
    rounds(
        1, 16,
        lambda i: greet(
            at(p, lax.rem(z + lax.div(i, 2), 8), lax.rem(c + lax.rem(i, 2), 2))
        ),
    )
    rounds(1, 4, lambda i: greet(at(y * 4 + lax.rem(x + i, 4), z, 1 - c)))

    def turn_in(src, dst):
        for j in range(D // 128):
            dst[j * 128 : (j + 1) * 128, :] = src[:, j * 128 : (j + 1) * 128].T

    inputs[0].wait()
    turn_in(values, val_t)
    pl.semaphore_wait(barrier, 33)

    def hop1(src, dst, ss, rs):
        local(src.at[pl.ds(p * 96, 96)], dst.at[p], rs.at[p])
        over_p(
            lambda q: remote(
                src.at[pl.ds(q * 96, 96)], dst.at[p], ss.at[q], rs.at[p], at(q, z, c)
            ).start()
        )

    def hop1_done(src, ss):
        over_p(lambda q: left(src.at[pl.ds(q * 96, 96)], ss.at[q]))

    hop1(val_t, r1v, s1vs, s1vr)

    inputs[1].wait()
    for j in range(D // 128):
        piece = queries[:, j * 128 : (j + 1) * 128].T
        for g in range(8):
            k = j * 8 + g
            qt[k // 12, (k // 3) % 4, (k % 3) * 16 : (k % 3) * 16 + 16, :] = (
                piece[g * 16 : g * 16 + 16]
            )
    inputs[2].wait()
    inputs[3].wait()

    def gated_rows(i):
        rows = pl.ds(pl.multiple_of(i * 256, 256), 256)
        g = dot_t(w_in[rows, :], out_grad[...])
        g_gated[rows, :] = g

    rounds(0, 6, gated_rows)
    gm_t[...] = (g_gated[...] * qt[...].reshape(D, TOK).astype(F32)).astype(BF16)

    inputs[4].wait()
    for part in range(2):
        turn_in(filt.at[part], fil_t.at[part])
    two = jnp.logical_or(n == 0, n == 3)
    sz = [
        lax.rem(z + 3 * (n == 2).astype(jnp.int32), 8),
        lax.rem(z + 8 + (n == 3).astype(jnp.int32) - (n == 0).astype(jnp.int32), 8),
    ]

    def unit_at(zz):
        return zz - (zz >= 3).astype(jnp.int32) - (zz >= 7).astype(jnp.int32)

    def f_src(k, q):
        return fil_t.at[:, pl.ds(q * 96 + unit_at(sz[k]) * 16, 16), :]

    def filter_hop1(k):
        local(f_src(k, p), f1.at[k, p], s1fr.at[k, p])
        over_p(
            lambda q: remote(
                f_src(k, q), f1.at[k, p], s1fs.at[k, q], s1fr.at[k, p], at(q, z, c)
            ).start()
        )

    filter_hop1(0)
    pl.when(two)(lambda: filter_hop1(1))
    hop1(gm_t, r1g, s1gs, s1gr)

    core = lax.div(n, 2)

    def z_of(u):
        return u + (u >= 2).astype(jnp.int32) + (u >= 5).astype(jnp.int32)

    def hop2(r1, r1_sem, dst, ss, rs):
        def row(j):
            yy = lax.rem(y + j, 4)
            blocks = pl.ds(yy * 4, 4)
            rounds(0, 4, lambda q: landed(r1.at[yy * 4 + q], r1_sem.at[yy * 4 + q]))
            slot = dst.at[lax.rem(n, 2), hc, blocks]
            sem = rs.at[lax.rem(n, 2), hc]

            def send(i):
                u = lax.rem(unit + i, 6)
                zz = z_of(u)
                src = r1.at[blocks, pl.ds(u * 16, 16), :]
                mine = jnp.logical_and(zz == z, core == c)

                @pl.when(mine)
                def _():
                    local(src, slot, sem)

                @pl.when(jnp.logical_not(mine))
                def _():
                    remote(src, slot, ss.at[u], sem, at(p, zz, core)).start()

            rounds(0, 6, send)

        rounds(0, 4, row)

    def hop2_done(r1, ss):
        def done(u):
            mine = jnp.logical_and(z_of(u) == z, core == c)

            @pl.when(jnp.logical_not(mine))
            def _():
                left(r1.at[:, pl.ds(u * 16, 16), :], ss.at[u])

        rounds(0, 6, done)

    hop2(r1v, s1vr, xv, s2vs, s2vr)

    def filter_hop2(k):
        rounds(0, 16, lambda q: landed(f1.at[k, q], s1fr.at[k, q]))
        mine = sz[k] == z

        @pl.when(mine)
        def _():
            local(f1.at[k], hx.at[h, c], s2fr.at[h])

        @pl.when(jnp.logical_not(mine))
        def _():
            remote(f1.at[k], hx.at[h, c], s2fs.at[k], s2fr.at[h], at(p, sz[k], c)).start()

    def filter_hop2_done(k):
        @pl.when(sz[k] != z)
        def _():
            left(f1.at[k], s2fs.at[k])

    filter_hop2(0)
    pl.when(two)(lambda: filter_hop2(1))
    hop2(r1g, s1gr, xg, s2gs, s2gr)

    other = at(p, z, 1 - c)

    def og_send(i):
        xx, cc = lax.rem(x + lax.div(i, 2), 4), lax.rem(c + lax.rem(i, 2), 2)
        half = pl.ds(pl.multiple_of(cc * 768, 768), 768)
        slot = og_all.at[x, pl.ds(pl.multiple_of(c * 128, 128), 128)]
        remote(
            out_grad.at[:, half], slot, s_ogs.at[i], s_ogr.at[x, c], at(y * 4 + xx, z, cc)
        ).start()

    def qx_send(i):
        xx = lax.rem(x + i, 4)
        remote(
            qt.at[:, xx], qx.at[x], s_qxs.at[i], s_qxr.at[x], at(y * 4 + xx, z, c)
        ).start()

    rounds(1, 4, qx_send)
    local(qt.at[:, x], qx.at[x], s_qxr.at[x])

    own_half = pl.ds(pl.multiple_of(c * 768, 768), 768)
    own_depth = pl.ds(pl.multiple_of(c * 128, 128), 128)
    local(out_grad.at[:, own_half], og_all.at[x, own_depth], s_ogr.at[x, c])
    rounds(1, 8, og_send)

    def transform(src, spec, nn):
        def get(hh, cc, yy, xx):
            return src[nn, 2 * hh + cc, 4 * yy + xx].astype(F32)

        def put(s, v):
            co, si = twist[0, s : s + 1, :], twist[1, s : s + 1, :]
            re, im = v
            if im is None:
                out = (re * co, -(re * si))
            else:
                out = (re * co + im * si, im * co - re * si)
            for j in range(2):
                hi, lo = split(out[j])
                lhi[s * 16 : s * 16 + 16, j * 128 : j * 128 + 128] = hi
                llo[s * 16 : s * 16 + 16, j * 128 : j * 128 + 128] = lo

        blocks_forward(get, put)
        spec[nn] = dot3(lhi[...], llo[...], m_fwd)

    def untransform(product, dst, nn):
        for j, v in enumerate(product):
            hi, lo = split(v)
            lhi[:, j * 128 : j * 128 + 128] = hi
            llo[:, j * 128 : j * 128 + 128] = lo
        back[...] = dot3(lhi[...], llo[...], m_inv)

        def get(s):
            co = twist[0, s : s + 1, :] * (1.0 / SEQ)
            si = twist[1, s : s + 1, :] * (1.0 / SEQ)
            re = back[s * 16 : s * 16 + 16, :128]
            im = back[s * 16 : s * 16 + 16, 128:]
            return (re * co - im * si, im * co + re * si)

        def put(hh, cc, yy, xx, v):
            dst[nn, 2 * hh + cc, 4 * yy + xx] = v.astype(BF16)

        blocks_inverse(get, put)

    def hop_a(src, dst, ss, rs, nn):
        def send(j):
            i = nn * 4 + j
            hh, cc = lax.rem(lax.div(i, 2), 2), lax.rem(i, 2)
            zz = hh * 4 + 2 * c + nn
            mine = jnp.logical_and(zz == z, cc == c)

            @pl.when(mine)
            def _():
                local(src.at[nn, 2 * hh + cc], dst.at[unit], rs.at[unit])

            @pl.when(jnp.logical_not(mine))
            def _():
                remote(
                    src.at[nn, 2 * hh + cc], dst.at[unit], ss.at[i], rs.at[unit], at(p, zz, cc)
                ).start()

        rounds(0, 4, send)

    def hop_a_done(src, ss):
        def done(i):
            nn, hh, cc = lax.div(i, 4), lax.rem(lax.div(i, 2), 2), lax.rem(i, 2)
            zz = hh * 4 + 2 * c + nn
            mine = jnp.logical_and(zz == z, cc == c)

            @pl.when(jnp.logical_not(mine))
            def _():
                left(src.at[nn, 2 * hh + cc], ss.at[i])

        rounds(0, 8, done)

    def hop_b(r2, r2_sem, dst, ss, rs):
        def relay(i):
            u = lax.rem(unit + i, 6)
            if r2_sem is not None:
                landed(r2.at[u], r2_sem.at[u])
            local(r2.at[u, p], dst.at[p, u], rs.at[p])
            over_p(
                lambda q: remote(
                    r2.at[u, q], dst.at[p, u], ss.at[q], rs.at[p], at(q, z, c)
                ).start()
            )

        rounds(0, 6, relay)

    def hop_b_done(r2, ss):
        over_p(lambda q: left(r2.at[:, q], ss.at[q]))

    ident = (
        lax.broadcasted_iota(jnp.int32, (128, 128), 0)
        == lax.broadcasted_iota(jnp.int32, (128, 128), 1)
    ).astype(F32).astype(BF16)
    flip = (
        lax.broadcasted_iota(jnp.int32, (128, 128), 0)
        == 127 - lax.broadcasted_iota(jnp.int32, (128, 128), 1)
    ).astype(F32).astype(BF16)

    for copy in inputs[5:]:
        copy.wait()

    @pl.when(active)
    def _():
        for hh in range(2):
            landed(hx.at[hh, c], s2fr.at[hh])
            remote(hx.at[hh, c], hx.at[hh, c], s3fs.at[hh], s3fr.at[hh], other).start()
        for hh in range(2):
            landed(hx.at[hh, 1 - c], s3fr.at[hh])

        def raw(k):
            return hx[(k >> 3) & 1, k & 1, (k >> 4) * 4 + ((k >> 1) & 3)]

        for k in HELD:
            s = slot_of(k)
            if k % 32:
                hrev[s * 32 : s * 32 + 32, :] = raw(64 - k).reshape(32, 128)
            else:
                hrev[s * 32 : s * 32 + 32, :] = jnp.zeros((32, 128), BF16)
        turned = dot(hrev[...], flip).reshape(SLOTS, 32, 128)
        for k in HELD:
            s = slot_of(k)
            v = raw(k).astype(F32)
            hs[s * 16 : s * 16 + 16, :128] = v[0] + turned[s, :16]
            hs[s * 16 : s * 16 + 16, 128:] = v[1] - turned[s, 16:]

        def values_part(nn):
            rounds(0, 4, lambda i: landed(xv.at[nn, i], s2vr.at[nn, i]))
            transform(xv, spec_v, nn)
            hr, hi = hs[:, :128], hs[:, 128:]
            vr, vi = spec_v[nn, :, :128], spec_v[nn, :, 128:]
            untransform((hr * vr - hi * vi, hr * vi + hi * vr), ymix, nn)
            hop_a(ymix, r2m, sams, samr, nn)

        rounds(0, 2, values_part)

        def grads_spectrum(nn):
            rounds(0, 4, lambda i: landed(xg.at[nn, i], s2gr.at[nn, i]))
            transform(xg, spec_g, nn)

        rounds(0, 2, grads_spectrum)
        re, im = 0.0, 0.0
        for nn in range(2):
            vr, vi = spec_v[nn, :, :128], spec_v[nn, :, 128:]
            gr_, gi = spec_g[nn, :, :128], spec_g[nn, :, 128:]
            re = re + (gr_ * vr + gi * vi)
            im = im + (gi * vr - gr_ * vi)
        gp[:, :128] = re * (1.0 / SEQ)
        gp[:, 128:] = im * (1.0 / SEQ)
        gp_rows = pl.ds(pl.multiple_of((1 - c) * 256, 256), 272)
        remote(gp.at[gp_rows], gpx, s_gps, s_gpr, other).start()

        landed(gpx, s_gpr)

        def fill(i):
            q, hh = lax.div(i, 2), lax.rem(i, 2)
            a = lax.div(q, 4) * 16 + hh * 8 + lax.rem(q, 4) * 2 + c
            low = lax.rem(a, 4)
            straight = jnp.logical_or(low == 1, jnp.logical_and(c == 0, a <= 32))
            k = jnp.where(straight, a, 64 - a)
            base = jnp.where(lax.rem(k, 4) == 1, 17, jnp.where(lax.rem(k, 4) == 2, 8, 0))
            s = jnp.where(k == 32, 16, base + lax.div(k, 4))
            total = gp[pl.ds(pl.multiple_of(s * 16, 16), 16), :] + gpx[
                pl.ds(pl.multiple_of(s * 16 - 256 * c, 16), 16), :
            ]
            gs[q, hh, 0] = total[:, :128].astype(BF16)
            gs[q, hh, 1] = total[:, 128:].astype(BF16)

        rounds(0, 32, fill)
        local(gs.at[p], gr.at[p], sagr.at[p])
        over_p(
            lambda q: remote(gs.at[q], gr.at[p], sags.at[q], sagr.at[p], at(q, z, c)).start()
        )

        def grads_part(nn):
            hr, hi = hs[:, :128], hs[:, 128:]
            gr_, gi = spec_g[nn, :, :128], spec_g[nn, :, 128:]
            untransform((gr_ * hr + gi * hi, gi * hr - gr_ * hi), ygv, nn)
            hop_a(ygv, r2v, savs, savr, nn)

        rounds(0, 2, grads_part)

    def mixed_share(i):
        u = lax.rem(unit + i, 6)
        landed(r2m.at[u], samr.at[u])
        xx = 2 * lax.rem(x, 2) + lax.div(u, 3)
        yh = y * 2 + lax.div(x, 2)
        slot = mx.at[:, yh, pl.ds(pl.multiple_of(lax.rem(u, 3) * 16, 16), 16), :]

        def send(j):
            yy = lax.rem(y + j, 4)
            src = r2m.at[u, pl.ds(yy * 4, 4)]
            mine = jnp.logical_and(j == 0, xx == x)

            @pl.when(mine)
            def _():
                local(src, slot, s_mxr.at[yh])

            @pl.when(jnp.logical_not(mine))
            def _():
                remote(
                    src, slot, s_mxs.at[u, yy], s_mxr.at[yh], at(yy * 4 + xx, z, c)
                ).start()

        rounds(0, 4, send)

    def mixed_share_done(u):
        xx = 2 * lax.rem(x, 2) + lax.div(u, 3)

        def done(yy):
            mine = jnp.logical_and(yy == y, xx == x)

            @pl.when(jnp.logical_not(mine))
            def _():
                left(r2m.at[u, pl.ds(yy * 4, 4)], s_mxs.at[u, yy])

        rounds(0, 4, done)

    hop1_done(val_t, s1vs)
    hop1_done(gm_t, s1gs)
    over_p(lambda q: left(f_src(0, q), s1fs.at[0, q]))
    filter_hop2_done(0)

    @pl.when(two)
    def _():
        over_p(lambda q: left(f_src(1, q), s1fs.at[1, q]))
        filter_hop2_done(1)

    hop2_done(r1v, s2vs)
    hop2_done(r1g, s2gs)
    rounds(1, 8, lambda i: left(og_all.at[x, own_depth], s_ogs.at[i]))
    rounds(1, 4, lambda i: left(qx.at[0], s_qxs.at[i]))

    rounds(0, 6, mixed_share)

    @pl.when(active)
    def _():
        rounds(0, 16, lambda q: landed(gr.at[q], sagr.at[q]))
        local(gr.at[:, h], gfi.at[:, unit], sbgr.at[unit])
        first = [
            h * 4 + jnp.where(n == 0, 1, jnp.where(n == 1, 0, 2)),
            h * 4 + jnp.where(n == 3, 1, 2),
            (1 - h) * 4 + jnp.where(n == 0, 1, 0),
            (1 - h) * 4 + jnp.where(n == 3, 2, 3),
        ]
        for k, zz in enumerate(first):
            half = h if k < 2 else 1 - h
            remote(
                gr.at[:, half], gfi.at[:, unit], sbgs.at[k], sbgr.at[unit], at(p, zz, c)
            ).start()

    rounds(0, 8, lambda i: landed(mx.at[:, i], s_mxr.at[i]))

    def gate(i):
        xx = lax.rem(x + i, 4)
        landed(qx.at[xx], s_qxr.at[xx])
        gat_all[xx, :, :, own_depth] = (qx[xx].astype(F32) * mx[xx].astype(F32)).astype(BF16)
        here = gat_all.at[xx, :, :, own_depth]
        remote(here, here, s_gxs.at[xx], s_gxr.at[xx], other).start()

    rounds(0, 4, gate)

    mate = h * 4 + n + 1 - 2 * lax.rem(n, 2)
    passes = [
        (h * 4 + 1, n == 2), (h * 4, n == 2), (h * 4 + 3, n == 1),
        ((1 - h) * 4 + 3, jnp.logical_or(n == 0, n == 2)),
        ((1 - h) * 4, jnp.logical_or(n == 1, n == 3)),
        ((1 - h) * 4 + 1, jnp.logical_or(n == 0, n == 3)),
    ]

    def gf_pass(k):
        source, here = passes[k]
        u = unit_at(source)

        @pl.when(here)
        def _():
            landed(gfi.at[:, u], sbgr.at[u])
            remote(
                gfi.at[:, u], gfi.at[:, u], sbgs.at[4 + k], sbgr.at[u], at(p, mate, c)
            ).start()

    def gf_last(k):
        source, here = passes[k]
        u = unit_at(source)

        @pl.when(jnp.logical_not(here))
        def _():
            landed(gfi.at[:, u], sbgr.at[u])

        pltpu.make_async_copy(gfi.at[:, u], o_gf.at[:, u], s_gfo.at[k]).start()

    def gf_left(k):
        source, here = passes[k]
        u = unit_at(source)

        @pl.when(here)
        def _():
            left(gfi.at[:, u], sbgs.at[4 + k])


    other_depth = pl.ds(pl.multiple_of((1 - c) * 128, 128), 128)

    def w_wait(xx):
        landed(gat_all.at[xx, :, :, other_depth], s_gxr.at[xx])
        landed(og_all.at[xx, own_depth], s_ogr.at[xx, c])
        landed(og_all.at[xx, other_depth], s_ogr.at[xx, 1 - c])

    rounds(0, 4, w_wait)

    def weight_rows(i):
        yy = lax.rem(y + i, 4)
        total = dot(gat_all[0, pl.ds(yy * 2, 2)].reshape(96, 256), og_all[0])
        for xx in range(1, 4):
            total = total + dot(gat_all[xx, pl.ds(yy * 2, 2)].reshape(96, 256), og_all[xx])
        wb[yy] = total.astype(BF16).reshape(2, 48, 768)

        @pl.when(i < 4)
        def _():
            remote(wb.at[yy], ry.at[y], srys.at[i], sryr.at[y], at(yy * 4 + x, z, c)).start()

    rounds(1, 5, weight_rows)
    hop_b(r2m, None, mix_t, sbms, sbmr)
    rounds(1, 4, lambda i: landed(ry.at[lax.rem(y + i, 4)], sryr.at[lax.rem(y + i, 4)]))
    total = wb[y].astype(F32)
    for i in range(1, 4):
        total = total + ry[lax.rem(y + i, 4)].astype(F32)
    sc[...] = total.astype(BF16).reshape(2, 3, 16, 768)

    def rc_send(i):
        hh, t = lax.div(i, 3), lax.rem(i, 3)
        zz = hh * 4 + t

        @pl.when(zz == z)
        def _():
            local(sc.at[hh, t], rc.at[z], srcr.at[z])

        @pl.when(zz != z)
        def _():
            remote(sc.at[hh, t], rc.at[z], srcs.at[i], srcr.at[z], at(p, zz, c)).start()

    rounds(0, 6, rc_send)
    hop_b(r2v, savr, gv_t, sbvs, sbvr)
    for k in range(6):
        gf_pass(k)
    rounds(0, 16, lambda q: landed(mix_t.at[q], sbmr.at[q]))
    gq = (g_gated[...] * mix_t[...].reshape(D, TOK).astype(F32)).astype(BF16)
    k_query[...] = dot_t(ident, gq).astype(BF16)
    query_out = pltpu.make_async_copy(k_query, o_query, s_out.at[0])
    query_out.start()

    rounds(0, 6, mixed_share_done)
    hop_b_done(r2m, sbms)
    rounds(0, 4, lambda i: left(gat_all.at[i, :, :, own_depth], s_gxs.at[i]))

    @pl.when(active)
    def _():
        for hh in range(2):
            left(hx.at[hh, c], s3fs.at[hh])
        hop_a_done(ymix, sams)
        hop_a_done(ygv, savs)
        left(gpx, s_gps)
        over_p(lambda q: left(gs.at[q], sags.at[q]))

    rounds(1, 4, lambda i: left(wb.at[0], srys.at[i]))
    rounds(0, 16, lambda q: landed(gv_t.at[q], sbvr.at[q]))
    k_value[...] = dot_t(ident, gv_t[...].reshape(D, TOK)).astype(BF16)
    value_out = pltpu.make_async_copy(k_value, o_value, s_out.at[1])
    value_out.start()
    owner = n < 3

    @pl.when(owner)
    def _():
        rounds(0, 8, lambda i: landed(rc.at[i], srcr.at[i]))
        total = rc[0].astype(F32)
        for i in range(1, 8):
            total = total + rc[i].astype(F32)
        sd[...] = total.astype(BF16)

        def send(i):
            nn, cc = lax.div(i, 2), lax.rem(i, 2)
            mine = jnp.logical_and(nn == n, cc == c)

            @pl.when(mine)
            def _():
                local(sd, rd.at[n, c], srdr.at[n, c])

            @pl.when(jnp.logical_not(mine))
            def _():
                remote(sd, rd.at[n, c], srds.at[i], srdr.at[n, c],
                       at(p, h * 4 + nn, cc)).start()

        rounds(0, 8, send)

    hop_b_done(r2v, sbvs)
    def rc_done(i):
        @pl.when(lax.div(i, 3) * 4 + lax.rem(i, 3) != z)
        def _():
            left(sd, srcs.at[i])

    rounds(0, 6, rc_done)

    for k in range(6):
        gf_last(k)
    for t in range(3):
        for cc in range(2):
            landed(rd.at[t, cc], srdr.at[t, cc])
    weight_out = pltpu.make_async_copy(rd, o_rd, s_out.at[3])
    weight_out.start()

    for copy in (query_out, value_out, weight_out):
        copy.wait()
    for k in range(6):
        left(gfi.at[:, 0], s_gfo.at[k])

    @pl.when(active)
    def _():
        rounds(0, 4, lambda k: left(gr.at[:, 0], sbgs.at[k]))

    for k in range(6):
        gf_left(k)

    @pl.when(owner)
    def _():
        def done(i):
            mine = jnp.logical_and(lax.div(i, 2) == n, lax.rem(i, 2) == c)

            @pl.when(jnp.logical_not(mine))
            def _():
                left(sd, srds.at[i])

        rounds(0, 8, done)


def finish(
    h_query, h_value, h_gf, h_rd, o_query, o_value, o_filter, o_weight,
    gfi, rd, k_query, k_value, k_filter, sem
):
    ctx = lax.axis_index("ctx")
    c = lax.rem(ctx, 2)
    gf_in = pltpu.make_async_copy(h_gf, gfi, sem.at[0])
    rd_in = pltpu.make_async_copy(h_rd, rd, sem.at[1])
    query_in = pltpu.make_async_copy(h_query, k_query, sem.at[2])
    value_in = pltpu.make_async_copy(h_value, k_value, sem.at[3])
    for copy in (gf_in, query_in, value_in, rd_in):
        copy.start()
    row = lax.broadcasted_iota(jnp.int32, (128, 128), 0)
    col = lax.broadcasted_iota(jnp.int32, (128, 128), 1)
    straight = jnp.logical_or(lax.rem(ctx, 4) == 1, jnp.logical_and(c == 0, ctx <= 32))
    pick = (row == jnp.where(straight, col, 127 - col)).astype(F32).astype(BF16)
    sign = jnp.where(straight, 1.0, -1.0)
    outs = [
        pltpu.make_async_copy(k_query, o_query, sem.at[6]),
        pltpu.make_async_copy(k_value, o_value, sem.at[7]),
    ]
    gf_in.wait()
    for copy, out in zip((query_in, value_in), outs):
        copy.wait()
        out.start()
    for part in range(2):
        value_part = dot_t(pick, gfi[:, :, part].reshape(D, TOK))
        k_filter[part] = value_part if part == 0 else value_part * sign
        out = pltpu.make_async_copy(k_filter.at[part], o_filter.at[part], sem.at[4 + part])
        out.start()
        outs.append(out)
    rd_in.wait()
    scale = 1.0 / math.sqrt(4 * SEQ)
    for cc in range(2):
        cols = slice(cc * 768, (cc + 1) * 768)

        @pl.when(c == 0)
        def _():
            o_weight[0:16, cols] = rd[0, cc].astype(F32) * scale
            o_weight[16:24, cols] = rd[1, cc].astype(F32)[0:8] * scale

        @pl.when(c == 1)
        def _():
            o_weight[0:8, cols] = rd[1, cc].astype(F32)[8:16] * scale
            o_weight[8:24, cols] = rd[2, cc].astype(F32) * scale

    for copy in outs:
        copy.wait()


def on_device(queries, values, out_grad, out_weight, filter_spec):
    m_fwd, m_inv, twist = tables()
    vmem = pl.BlockSpec(memory_space=pltpu.VMEM)
    dma = pltpu.SemaphoreType.DMA

    def held(*shape, dtype=BF16):
        return pltpu.VMEM(shape, dtype)

    scratch = [
        held(TOK, D), held(TOK, D), held(TOK, D), held(D, D), held(2, TOK, D),
        held(2, 256, 256), held(2, 256, 256), held(2, 40, TOK, dtype=F32),
        held(D, TOK, dtype=F32), held(8, 4, 48, TOK), held(D, TOK), held(D, TOK), held(2, D, TOK),
        held(16, 96, TOK), held(16, 96, TOK), held(2, 16, 2, 16, TOK),
        held(2, 4, 16, 16, TOK), held(2, 4, 16, 16, TOK), held(2, 2, 16, 2, 16, TOK),
        held(SLOTS * 32, TOK), held(ROWS, 256, dtype=F32),
        held(ROWS, 256), held(ROWS, 256),
        held(2, ROWS, 256, dtype=F32), held(2, ROWS, 256, dtype=F32), held(ROWS, 256, dtype=F32),
        held(2, 4, 16, 16, TOK), held(2, 4, 16, 16, TOK),
        held(6, 16, 16, TOK), held(6, 16, 16, TOK),
        held(16, 6, 16, TOK), held(16, 6, 16, TOK),
        held(ROWS, 256, dtype=F32), held(272, 256, dtype=F32),
        held(16, 2, 2, 16, TOK), held(16, 2, 2, 16, TOK), held(16, 6, 2, 16, TOK),
        held(TOK, D), held(TOK, D), dma((4,)), dma((6,)),
        held(4, 8, 48, TOK), held(4, 8, 48, TOK), held(4, 256, 768), held(4, 8, 48, 256),
        held(4, 2, 48, 768), held(4, 2, 48, 768),
        held(2, 3, 16, 768), held(8, 16, 768), held(16, 768), held(3, 2, 16, 768),
        dma((8,)), dma((8,)), dma((4, 2)), dma((4,)), dma((4,)), dma((6, 4)), dma((8,)), dma((4,)),
        dma((4,)), dma, dma,
        dma((16,)), dma((16,)), dma((16,)), dma((16,)), dma((2, 16)), dma((2, 16)),
        dma((6,)), dma((2, 4)), dma((6,)), dma((2, 4)), dma((2,)), dma((2,)), dma((2,)), dma((2,)),
        dma((8,)), dma((6,)), dma((8,)), dma((6,)), dma((16,)), dma((16,)), dma((16,)), dma((16,)),
        dma((16,)), dma((16,)), dma((10,)), dma((6,)),
        dma((4,)), dma((4,)), dma((6,)), dma((8,)), dma((8,)), dma((3, 2)),
    ]
    anywhere = pl.BlockSpec(memory_space=pl.ANY)
    parts = pl.pallas_call(
        kernel,
        out_shape=(
            jax.ShapeDtypeStruct((TOK, D), BF16),
            jax.ShapeDtypeStruct((TOK, D), BF16),
            jax.ShapeDtypeStruct((16, 6, 2, 16, TOK), BF16),
            jax.ShapeDtypeStruct((3, 2, 16, 768), BF16),
        ),
        in_specs=[pl.BlockSpec(memory_space=pl.ANY)] * 8,
        out_specs=(anywhere,) * 4,
        scratch_shapes=scratch,
        compiler_params=pltpu.CompilerParams(
            collective_id=0, has_side_effects=True, vmem_limit_bytes=60 * 2**20
        ),
    )(values[0], queries[0], out_grad[0], out_weight, filter_spec,
      jnp.asarray(m_fwd), jnp.asarray(m_inv), jnp.asarray(twist))
    grad_query, grad_value, grad_filter, grad_weight = pl.pallas_call(
        finish,
        out_shape=(
            jax.ShapeDtypeStruct((TOK, D), BF16),
            jax.ShapeDtypeStruct((TOK, D), BF16),
            jax.ShapeDtypeStruct((2, TOK, D), F32),
            jax.ShapeDtypeStruct((24, D), F32),
        ),
        in_specs=[anywhere] * 4,
        out_specs=(anywhere, anywhere, anywhere, vmem),
        scratch_shapes=[
            held(16, 6, 2, 16, TOK), held(3, 2, 16, 768), held(TOK, D), held(TOK, D),
            held(2, TOK, D, dtype=F32), dma((8,)),
        ],
        compiler_params=pltpu.CompilerParams(vmem_limit_bytes=60 * 2**20),
    )(*parts)
    return grad_query[None], grad_value[None], grad_filter, grad_weight


def solution(mesh):
    return jax.shard_map(
        on_device,
        mesh=mesh,
        in_specs=(
            P("dp", "ctx", None),
            P("dp", "ctx", None),
            P("dp", "ctx", None),
            P(),
            P(None, "ctx", None),
        ),
        out_specs=(
            P("dp", "ctx", None),
            P("dp", "ctx", None),
            P(None, "ctx", None),
            P("ctx", None),
        ),
        check_vma=False,
    )
```
